512 devices in a mesh: dp: 16 (over z), replica: 8 (over y_lo, x), tensor: 4 (over y_hi, core).
Axes of the slice: x: 4, y: 4 (y_hi: 2, y_lo: 2; y = y_hi * 2 + y_lo), z: 16, core: 2. Of those that a mesh axis runs over, the one named last changes fastest.
Arguments:
- image_residual_input: bfloat16 [16384, 1152], P(('dp', 'replica')), may hold values from -6 to 6
- image_hidden_units: bfloat16 [16384, 2176], P(('dp', 'replica'), 'tensor'), may hold values from -12 to 12, as said below
- image_output_weight: bfloat16 [2176, 1152], P('tensor'), may hold values from -0.125 to 0.125
- text_residual_input: bfloat16 [16384, 1152], P(('dp', 'replica')), may hold values from -6 to 6
- text_hidden_units: bfloat16 [16384, 2176], P(('dp', 'replica'), 'tensor'), may hold values from -12 to 12, as said below
- text_output_weight: bfloat16 [2176, 1152], P('tensor'), may hold values from -0.125 to 0.125
- log_logit_scale: float32 [1], replicated, may hold values from 1.8 to 2.6
- pair_logit_bias: float32 [1], replicated, may hold values from -4 to -1
Outputs:
- hidden_grad_image: bfloat16 [16384, 2176], P(('dp', 'replica'), 'tensor')
- hidden_grad_text: bfloat16 [16384, 2176], P(('dp', 'replica'), 'tensor')
- weight_grad_image: float32 [2176, 1152], P('tensor', 'replica')
- weight_grad_text: float32 [2176, 1152], P('tensor', 'replica')
The draws below stay inside these ranges and needn't reach their ends.
Inputs may be any that keep to these rules, and one draw needn't show every extreme that they name: `image_hidden_units`: post-activation hidden values; each row has its own scale. `text_hidden_units`: post-activation hidden values; each row has its own scale.
All inputs are finite; a program needn't handle non-finite values.
Results may differ from the reference program's by a relative error of at most 0.022.
Values may be sent and summed in bfloat16 or wider, within the bound.
No kernel may reach another device: no remote copies, remote signals or barrier semaphores. Data moves between devices by JAX's collectives and lax.ppermute only.
A program may use at most 64 MiB of HBM per device.

```python
import math
import jax
import jax.numpy as jnp
from jax import lax

D = 1152
HID = 2176
TOK_DEV = 128
PIECE = 64
TOKENS = 16384
N_DP = 16
N_REPLICA = 8
N_TENSOR = 4


def shared_structure(key, strength, offset):
    pieces = jax.random.split(key, 3)
    basis_rows = jax.random.normal(pieces[0], (4, D), jnp.float32)
    latent = jax.random.normal(pieces[1], (TOKENS, 4), jnp.float32)
    common = jax.random.normal(pieces[2], (1, D), jnp.float32)
    running_sum = offset * common
    for column in range(4):
        running_sum = running_sum + 0.5 * strength * latent[:, column:column + 1] * basis_rows[column:column + 1, :]
    return running_sum


def draw_image_residual_input(key, part):
    shared = shared_structure(key, 1.5, 0.0)
    key = jax.random.fold_in(key, 31)
    noise_values = jax.random.truncated_normal(key, -4.0, 4.0, (TOKENS, D), jnp.float32)
    return jnp.clip(shared + noise_values, -6.0, 6.0).astype(jnp.bfloat16)


def draw_text_residual_input(key, part):
    shared = shared_structure(key, 1.5, 0.0)
    key = jax.random.fold_in(key, 47)
    noise_values = jax.random.truncated_normal(key, -4.0, 4.0, (TOKENS, D), jnp.float32)
    return jnp.clip(shared + noise_values, -6.0, 6.0).astype(jnp.bfloat16)


def draw_image_hidden_units(key, part):
    key = jax.random.fold_in(key, 11)
    subkeys = jax.random.split(key, 2)
    noise_values = jax.random.truncated_normal(subkeys[0], -4.0, 4.0, (TOKENS, HID), jnp.float32)
    scales = jnp.exp(jax.random.uniform(subkeys[1], (TOKENS, 1), jnp.float32, math.log(0.3), math.log(3.0)))
    return (noise_values * scales).astype(jnp.bfloat16)


def draw_text_hidden_units(key, part):
    key = jax.random.fold_in(key, 23)
    subkeys = jax.random.split(key, 2)
    noise_values = jax.random.truncated_normal(subkeys[0], -4.0, 4.0, (TOKENS, HID), jnp.float32)
    scales = jnp.exp(jax.random.uniform(subkeys[1], (TOKENS, 1), jnp.float32, math.log(0.3), math.log(3.0)))
    return (noise_values * scales).astype(jnp.bfloat16)


def block_scale(rng, dims, cuts, smallest, high):
    def one(axis_at, shards_of):
        heights = jax.random.uniform(jax.random.fold_in(jax.random.fold_in(rng, 6), axis_at), (shards_of,), jnp.float32, smallest / len(cuts), high / len(cuts))
        return jnp.repeat(jnp.exp(heights), dims[axis_at] // shards_of).reshape((-1,) + (1,) * (len(dims) - axis_at - 1))

    loudness = one(*cuts[0])
    for cut in cuts[1:]:
        loudness = loudness * one(*cut)
    return loudness


def gaussian(stream_key, extent, width, limit, cuts=(), kind=jnp.bfloat16):
    values = width * jax.random.normal(stream_key, extent, jnp.float32)
    if cuts:
        values = values * block_scale(stream_key, extent, cuts, -0.22, 0.18)
    return jnp.clip(values, -limit, limit).astype(kind)


def setup_inputs(seed: int = 0) -> dict:
    key_of = jax.random.split(jax.random.key(seed), 9)
    image_residual_input = draw_image_residual_input(jax.random.fold_in(key_of[8], 71), 0)
    image_hidden_units = draw_image_hidden_units(jax.random.fold_in(key_of[8], 71), 0)
    image_output_weight = gaussian(key_of[2], (HID, D), HID ** -0.5, 0.125, ((0, 4),))
    text_residual_input = draw_text_residual_input(jax.random.fold_in(key_of[8], 71), 0)
    text_hidden_units = draw_text_hidden_units(jax.random.fold_in(key_of[8], 71), 0)
    text_output_weight = gaussian(key_of[5], (HID, D), HID ** -0.5, 0.125, ((0, 4),))
    log_logit_scale = jnp.clip(jax.random.uniform(key_of[6], (1,), jnp.float32, 1.8, 2.6), 1.8, 2.6)
    pair_logit_bias = jnp.clip(jax.random.uniform(key_of[7], (1,), jnp.float32, -4.0, -1.0), -4.0, -1.0)
    return dict(image_residual_input=image_residual_input, image_hidden_units=image_hidden_units, image_output_weight=image_output_weight, text_residual_input=text_residual_input, text_hidden_units=text_hidden_units, text_output_weight=text_output_weight, log_logit_scale=log_logit_scale, pair_logit_bias=pair_logit_bias)


def tower_output(residual, hidden, weight):
    slice_width = HID // N_TENSOR
    running = jnp.zeros(residual.shape, jnp.float32)
    for column in range(N_TENSOR):
        product = jnp.dot(hidden[:, column * slice_width:(column + 1) * slice_width], weight[column * slice_width:(column + 1) * slice_width], preferred_element_type=jnp.float32).astype(jnp.bfloat16)
        running = running + lax.optimization_barrier(product).astype(jnp.float32)
    combined = residual.astype(jnp.float32) + running
    inverse = lax.rsqrt(lax.optimization_barrier(jnp.sum(combined * combined, axis=1, keepdims=True)) + 1e-06)
    return (combined * inverse, inverse)

def retract(normed, inverse, gradient):
    projection = lax.optimization_barrier(jnp.sum(normed * gradient, axis=1, keepdims=True))
    return ((gradient - normed * projection) * inverse).astype(jnp.bfloat16)

def weight_grad(hidden, upstream):
    groups = N_DP * N_REPLICA
    hidden_groups = hidden.reshape(groups, TOK_DEV, HID)
    upstream_groups = upstream.reshape(groups, TOK_DEV, D)

    def accumulate(running, group_pair):
        product = jnp.dot(group_pair[0].T, group_pair[1], preferred_element_type=jnp.float32).astype(jnp.bfloat16)
        return (running + lax.optimization_barrier(product).astype(jnp.float32), None)
    running, unused = lax.scan(accumulate, jnp.zeros((HID, D), jnp.float32), (hidden_groups, upstream_groups))
    return running

def reference(image_residual_input, image_hidden_units, image_output_weight, text_residual_input, text_hidden_units, text_output_weight, log_logit_scale, pair_logit_bias):
    normed_image, inverse_image = tower_output(image_residual_input, image_hidden_units, image_output_weight)
    normed_text, inverse_text = tower_output(text_residual_input, text_hidden_units, text_output_weight)
    embed_image = normed_image.astype(jnp.bfloat16)
    text_embedding_output = normed_text.astype(jnp.bfloat16)
    logit_scale_value = jnp.exp(log_logit_scale[0])
    shifted_logit_bias = pair_logit_bias[0]
    block_rows = math.gcd(TOKENS, 512)
    block_count = TOKENS // block_rows
    text_label_index = jnp.arange(TOKENS, dtype=jnp.int32)
    text_classes = text_embedding_output.astype(jnp.float32).reshape(N_DP, N_REPLICA, 2, PIECE, D)

    def visit_block(text_running, block_index):
        first_row = block_index * block_rows
        image_row_block = lax.dynamic_slice_in_dim(embed_image, first_row, block_rows, 0)
        pair_logit_matrix = logit_scale_value * jnp.dot(image_row_block, text_embedding_output.T, preferred_element_type=jnp.float32) + shifted_logit_bias
        matches = (first_row + jnp.arange(block_rows, dtype=jnp.int32))[:, None] == text_label_index[None, :]
        label_sign_matrix = jnp.where(matches, 1.0, -1.0).astype(jnp.float32)
        pair_coefficients = (-label_sign_matrix * jax.nn.sigmoid(-label_sign_matrix * pair_logit_matrix) * logit_scale_value).astype(jnp.bfloat16)
        class_sums = jnp.einsum('idrgk,drgkc->irgc', pair_coefficients.astype(jnp.float32).reshape(block_rows, N_DP, N_REPLICA, 2, PIECE), text_classes)
        rounded = lax.optimization_barrier(class_sums.astype(jnp.bfloat16)).astype(jnp.float32)
        image_block = lax.optimization_barrier(jnp.sum(rounded, axis=(1, 2)))
        text_running = text_running + jnp.dot(pair_coefficients.T, image_row_block, preferred_element_type=jnp.float32)
        return (text_running, image_block)
    text_grad, image_blocks = lax.scan(visit_block, jnp.zeros((TOKENS, D), jnp.float32), jnp.arange(block_count, dtype=jnp.int32))
    image_grad = image_blocks.reshape(TOKENS, D)
    upstream_image = retract(normed_image, inverse_image, image_grad)
    upstream_text = retract(normed_text, inverse_text, text_grad)
    hidden_grad_image = jnp.dot(upstream_image, image_output_weight.T, preferred_element_type=jnp.float32).astype(jnp.bfloat16)
    hidden_grad_text = jnp.dot(upstream_text, text_output_weight.T, preferred_element_type=jnp.float32).astype(jnp.bfloat16)
    weight_grad_image = weight_grad(image_hidden_units, upstream_image)
    weight_grad_text = weight_grad(text_hidden_units, upstream_text)
    return (hidden_grad_image, hidden_grad_text, weight_grad_image, weight_grad_text)
```

```python
import jax
import jax.numpy as jnp
from jax import lax
from jax.sharding import PartitionSpec as P

F32 = jnp.float32
BF16 = jnp.bfloat16
PLANE = ("replica", "tensor")


def dot(a, b, contract):
    return lax.dot_general(a, b, (contract, ((), ())), preferred_element_type=F32)


def exchange(x, axis):
    return lax.all_to_all(x, axis, split_axis=0, concat_axis=0, tiled=True)


def spread(x, axis):
    size = lax.axis_size(axis)
    return exchange(jnp.broadcast_to(x[None], (size,) + x.shape), axis)


def after(x, *others):
    return lax.optimization_barrier((x,) + others)[0]


def normalize(residual, summed):
    combined = residual.astype(F32) + summed
    inverse = lax.rsqrt(jnp.sum(combined * combined, axis=1, keepdims=True) + 1e-06)
    return (combined * inverse, inverse)


def retract(normed, inverse, gradient):
    projection = jnp.sum(normed * gradient, axis=1, keepdims=True)
    return ((gradient - normed * projection) * inverse).astype(BF16)


def shards(
    image_residual_input,
    image_hidden_units,
    image_output_weight,
    text_residual_input,
    text_hidden_units,
    text_output_weight,
    log_logit_scale,
    pair_logit_bias,
):
    rows, width = image_residual_input.shape
    hidden = image_hidden_units.shape[1]
    n_dp = lax.axis_size("dp")
    n_replica = lax.axis_size("replica")
    n_tensor = lax.axis_size("tensor")
    dp = lax.axis_index("dp")
    replica = lax.axis_index("replica")
    tensor = lax.axis_index("tensor")
    own = rows // n_tensor
    members = n_replica * n_tensor
    columns = width // n_replica

    terms = jnp.concatenate(
        [
            dot(image_hidden_units, image_output_weight, ((1,), (0,)))
            .astype(BF16)
            .reshape(n_tensor, own, width),
            dot(text_hidden_units, text_output_weight, ((1,), (0,)))
            .astype(BF16)
            .reshape(n_tensor, own, width),
        ],
        axis=1,
    )
    summed = jnp.sum(exchange(terms, "tensor").astype(F32), axis=0)
    image_residual = lax.dynamic_slice_in_dim(image_residual_input, tensor * own, own, 0)
    text_residual = lax.dynamic_slice_in_dim(text_residual_input, tensor * own, own, 0)
    normed_text, inverse_text = normalize(text_residual, summed[own:])
    normed_image, inverse_image = normalize(image_residual, summed[:own])

    texts = lax.all_gather(normed_text.astype(BF16), "dp", axis=0, tiled=True)
    images = spread(normed_image.astype(BF16), PLANE)
    hidden_image = spread(after(image_hidden_units, images), "replica")
    texts, images, hidden_image = lax.optimization_barrier((texts, images, hidden_image))
    images = images.reshape(members * own, width)

    scale = jnp.exp(log_logit_scale[0])
    logits = scale * dot(images, texts, ((1,), (1,))) + pair_logit_bias[0]
    image_index = dp * (members * own) + jnp.arange(members * own, dtype=jnp.int32)
    position = jnp.arange(n_dp * own, dtype=jnp.int32)
    text_index = (
        (position // own) * (members * own)
        + (replica * n_tensor + tensor) * own
        + position % own
    )
    label = jnp.where(image_index[:, None] == text_index[None, :], 1.0, -1.0).astype(F32)
    coefficients = (-label * jax.nn.sigmoid(-label * logits) * scale).astype(BF16)
    text_partial = dot(coefficients, images, ((0,), (0,))).astype(BF16)
    image_partial = dot(coefficients, texts, ((1,), (0,))).astype(BF16)

    text_grad = lax.psum_scatter(text_partial, "dp", scatter_dimension=0, tiled=True).astype(F32)
    image_parts = exchange(image_partial.reshape(members, own, width), PLANE)
    image_grad = jnp.sum(image_parts.astype(F32), axis=0)
    hidden_text = spread(after(text_hidden_units, image_parts), "replica")
    text_grad, image_grad, hidden_text = lax.optimization_barrier(
        (text_grad, image_grad, hidden_text)
    )

    upstream = jnp.concatenate(
        [
            retract(normed_image, inverse_image, image_grad),
            retract(normed_text, inverse_text, text_grad),
        ],
        axis=0,
    )
    group = lax.all_gather(upstream, "tensor", axis=0).reshape(n_tensor, 2, own, width)
    hidden_grad_image = dot(
        group[:, 0].reshape(rows, width), image_output_weight, ((1,), (1,))
    ).astype(BF16)
    hidden_grad_text = dot(
        group[:, 1].reshape(rows, width), text_output_weight, ((1,), (1,))
    ).astype(BF16)

    cut = jnp.transpose(upstream.reshape(2 * own, n_replica, columns), (1, 0, 2))
    cut = jnp.broadcast_to(cut[:, None], (n_replica, n_tensor, 2 * own, columns))
    cut = exchange(cut.reshape(members, 2 * own, columns), PLANE)
    cut_image = cut[:, :own].reshape(members * own, columns)
    cut_text = cut[:, own:].reshape(members * own, columns)
    partial = jnp.concatenate(
        [
            dot(hidden_image.reshape(members * own, hidden), cut_image, ((0,), (0,))),
            dot(hidden_text.reshape(members * own, hidden), cut_text, ((0,), (0,))),
        ],
        axis=1,
    ).astype(BF16)
    pieces = exchange(partial.reshape(n_dp, hidden // n_dp, 2 * columns), "dp")
    share = jnp.sum(pieces.astype(F32), axis=0).astype(BF16)
    total = spread(share, "dp").reshape(hidden, 2 * columns).astype(F32)
    return (hidden_grad_image, hidden_grad_text, total[:, :columns], total[:, columns:])


def solution(mesh):
    in_specs = (
        P(("dp", "replica"), None),
        P(("dp", "replica"), "tensor"),
        P("tensor", None),
        P(("dp", "replica"), None),
        P(("dp", "replica"), "tensor"),
        P("tensor", None),
        P(),
        P(),
    )
    out_specs = (
        P(("dp", "replica"), "tensor"),
        P(("dp", "replica"), "tensor"),
        P("tensor", "replica"),
        P("tensor", "replica"),
    )
    return jax.shard_map(shards, mesh=mesh, in_specs=in_specs, out_specs=out_specs, check_vma=False)
```

```python
import jax
import jax.numpy as jnp
from jax import lax
from jax.sharding import PartitionSpec as P

F32 = jnp.float32
BF16 = jnp.bfloat16
PLANE = ("replica", "tensor")


def dot(a, b, contract):
    return lax.dot_general(a, b, (contract, ((), ())), preferred_element_type=F32)


def exchange(x, axis):
    return lax.all_to_all(x, axis, split_axis=0, concat_axis=0, tiled=True)


def spread(x, axis):
    size = lax.axis_size(axis)
    return exchange(jnp.broadcast_to(x[None], (size,) + x.shape), axis)


def after(x, *others):
    return lax.optimization_barrier((x,) + others)[0]


OFFSETS = (0, -4, -8, -12, -1, -5, -9, -13, 1, -3, -7, -11, 2, -2, -6, -10)
PLACES = tuple([offset % 16 for offset in OFFSETS].index(k) for k in range(16))


def shift(x, by):
    size = lax.axis_size("dp")
    return lax.ppermute(x, "dp", [(i, (i + by) % size) for i in range(size)])


def gather_dp(x):
    half = x.shape[0] // 16 * 8
    below = shift(x, 4)
    above = shift(x, -4)
    far = jnp.concatenate([shift(above[:half], -4), shift(below[half:], 4)], axis=0)
    quad = jnp.stack([x, below, far, above])
    return jnp.concatenate(
        [quad, shift(quad, 1), shift(quad, -1), shift(quad[0:2], -2), shift(quad[1:3], 2)],
        axis=0,
    )


def scatter_dp(x):
    half = x.shape[1] // 16 * 8
    one = shift(x[4:8], -1)
    two = shift(x[8:12], 1)
    three = shift(x[12:14], 2)
    four = shift(x[14:16], -2)
    quad = x[0:4].astype(F32) + one.astype(F32) + two.astype(F32)
    near = quad[0] + three[0].astype(F32)
    below = quad[1] + three[1].astype(F32) + four[0].astype(F32)
    far = (quad[2] + four[1].astype(F32)).astype(BF16)
    above = quad[3]
    above_half = shift(far[:half], 4).astype(F32)
    below_half = shift(far[half:], -4).astype(F32)
    above = jnp.concatenate([above[:half] + above_half, above[half:]], axis=0).astype(BF16)
    below = jnp.concatenate([below[:half], below[half:] + below_half], axis=0).astype(BF16)
    return near + shift(above, 4).astype(F32) + shift(below, -4).astype(F32)


def chunked(hidden_units, dp, size):
    rows, hidden = hidden_units.shape
    chunk = hidden // size
    slots = -(-chunk // 8) * 8
    x = hidden_units.T.reshape(size, chunk, rows)
    x = lax.optimization_barrier(jnp.pad(x, ((0, 0), (0, slots - chunk), (0, 0))))
    place = (dp + jnp.array(OFFSETS, jnp.int32)) % size
    return x.at[place].get(mode="promise_in_bounds").reshape(size * slots, rows)


def normalize(residual, summed):
    combined = residual.astype(F32) + summed
    inverse = lax.rsqrt(jnp.sum(combined * combined, axis=1, keepdims=True) + 1e-06)
    return (combined * inverse, inverse)


def retract(normed, inverse, gradient):
    projection = jnp.sum(normed * gradient, axis=1, keepdims=True)
    return ((gradient - normed * projection) * inverse).astype(BF16)


def shards(
    image_residual_input,
    image_hidden_units,
    image_output_weight,
    text_residual_input,
    text_hidden_units,
    text_output_weight,
    log_logit_scale,
    pair_logit_bias,
):
    rows, width = image_residual_input.shape
    hidden = image_hidden_units.shape[1]
    n_dp = lax.axis_size("dp")
    n_replica = lax.axis_size("replica")
    n_tensor = lax.axis_size("tensor")
    dp = lax.axis_index("dp")
    replica = lax.axis_index("replica")
    tensor = lax.axis_index("tensor")
    own = rows // n_tensor
    members = n_replica * n_tensor
    columns = width // n_replica

    terms = jnp.concatenate(
        [
            dot(image_hidden_units, image_output_weight, ((1,), (0,)))
            .astype(BF16)
            .reshape(n_tensor, own, width),
            dot(text_hidden_units, text_output_weight, ((1,), (0,)))
            .astype(BF16)
            .reshape(n_tensor, own, width),
        ],
        axis=1,
    )
    summed = jnp.sum(exchange(terms, "tensor").astype(F32), axis=0)
    image_residual = lax.dynamic_slice_in_dim(image_residual_input, tensor * own, own, 0)
    text_residual = lax.dynamic_slice_in_dim(text_residual_input, tensor * own, own, 0)
    normed_text, inverse_text = normalize(text_residual, summed[own:])
    normed_image, inverse_image = normalize(image_residual, summed[:own])

    images = spread(normed_image.astype(BF16), PLANE)
    texts = gather_dp(normed_text.astype(BF16))
    hidden_text = spread(chunked(text_hidden_units, dp, n_dp), "replica")
    texts, images, hidden_text = lax.optimization_barrier((texts, images, hidden_text))
    texts = texts.reshape(n_dp * own, width)
    images = images.reshape(members * own, width)
    hidden_image = spread(after(chunked(image_hidden_units, dp, n_dp), images), "replica")

    scale = jnp.exp(log_logit_scale[0])
    logits = scale * dot(images, texts, ((1,), (1,))) + pair_logit_bias[0]
    image_index = jnp.arange(members * own, dtype=jnp.int32)
    position = jnp.arange(n_dp * own, dtype=jnp.int32)
    text_index = jnp.where(position < own, (replica * n_tensor + tensor) * own + position, -1)
    label = jnp.where(image_index[:, None] == text_index[None, :], 1.0, -1.0).astype(F32)
    coefficients = (-label * jax.nn.sigmoid(-label * logits) * scale).astype(BF16)
    text_partial = dot(coefficients, images, ((0,), (0,))).astype(BF16)
    image_partial = dot(after(coefficients, text_partial), texts, ((1,), (0,))).astype(BF16)
    image_partial, hidden_image = lax.optimization_barrier((image_partial, hidden_image))

    text_grad = scatter_dp(text_partial.reshape(n_dp, own, width))
    image_parts = exchange(image_partial.reshape(members, own, width), PLANE)
    image_grad = jnp.sum(image_parts.astype(F32), axis=0)

    upstream_image = retract(normed_image, inverse_image, image_grad)
    upstream_text = retract(normed_text, inverse_text, text_grad)
    cut = jnp.concatenate(
        [
            upstream_image.reshape(own, n_replica, columns),
            upstream_text.reshape(own, n_replica, columns),
        ],
        axis=2,
    )
    cut = jnp.transpose(cut, (1, 0, 2))
    cut = jnp.broadcast_to(cut[:, None], (n_replica, n_tensor, own, 2 * columns))
    cut = exchange(cut.reshape(members, own, 2 * columns), PLANE)
    cut = cut.reshape(members * own, 2 * columns)
    slots = hidden_image.shape[1]
    hidden_image = jnp.transpose(hidden_image, (1, 0, 2)).reshape(slots, members * own)
    hidden_text = jnp.transpose(hidden_text, (1, 0, 2)).reshape(slots, members * own)
    partial = jnp.where(
        jnp.arange(2 * columns)[None, :] < columns,
        dot(hidden_image, cut, ((1,), (0,))),
        dot(hidden_text, cut, ((1,), (0,))),
    ).astype(BF16)
    share = scatter_dp(partial.reshape(n_dp, slots // n_dp, 2 * columns)).astype(BF16)
    total = gather_dp(share)

    group = lax.all_gather(jnp.stack([upstream_image, upstream_text]), "tensor", axis=1)
    hidden_grad_image = dot(
        group[0].reshape(rows, width), image_output_weight, ((1,), (1,))
    ).astype(BF16)
    hidden_grad_text = dot(
        group[1].reshape(rows, width), text_output_weight, ((1,), (1,))
    ).astype(BF16)

    place = jnp.array(PLACES, jnp.int32)[(jnp.arange(n_dp, dtype=jnp.int32) - dp) % n_dp]
    total = lax.optimization_barrier(total).at[place].get(mode="promise_in_bounds")
    total = total[:, : hidden // n_dp].astype(F32)
    total = total.reshape(hidden, 2 * columns)
    return (hidden_grad_image, hidden_grad_text, total[:, :columns], total[:, columns:])


def solution(mesh):
    in_specs = (
        P(("dp", "replica"), None),
        P(("dp", "replica"), "tensor"),
        P("tensor", None),
        P(("dp", "replica"), None),
        P(("dp", "replica"), "tensor"),
        P("tensor", None),
        P(),
        P(),
    )
    out_specs = (
        P(("dp", "replica"), "tensor"),
        P(("dp", "replica"), "tensor"),
        P("tensor", "replica"),
        P("tensor", "replica"),
    )
    return jax.shard_map(shards, mesh=mesh, in_specs=in_specs, out_specs=out_specs, check_vma=False)
```

```python
import math

import jax
import jax.numpy as jnp
from jax import lax
from jax.sharding import Mesh
from jax.sharding import PartitionSpec as P

F32 = jnp.float32
BF16 = jnp.bfloat16
PLANE = ("replica", "tensor")


def dot(a, b, contract):
    return lax.dot_general(a, b, (contract, ((), ())), preferred_element_type=F32)


def exchange(x, axis):
    return lax.all_to_all(x, axis, split_axis=0, concat_axis=0, tiled=True)


def spread(x, axis):
    size = lax.axis_size(axis)
    return exchange(jnp.broadcast_to(x[None], (size,) + x.shape), axis)


def after(x, *others):
    return lax.optimization_barrier((x,) + others)[0]


def gather_dp(x):
    runs = lax.all_gather(x, "run", axis=0)
    return spread(runs, "place")


def scatter_dp(x):
    runs = jnp.sum(exchange(x, "place").astype(F32), axis=0).astype(BF16)
    return jnp.sum(exchange(runs, "run").astype(F32), axis=0)


def chunked(hidden_units, size):
    rows, hidden = hidden_units.shape
    chunk = hidden // size
    slots = -(-chunk // 8) * 8
    x = hidden_units.T.reshape(size, chunk, rows)
    return jnp.pad(x, ((0, 0), (0, slots - chunk), (0, 0))).reshape(size * slots, rows)


def normalize(residual, summed):
    combined = residual.astype(F32) + summed
    inverse = lax.rsqrt(jnp.sum(combined * combined, axis=1, keepdims=True) + 1e-06)
    return (combined * inverse, inverse)


def retract(normed, inverse, gradient):
    projection = jnp.sum(normed * gradient, axis=1, keepdims=True)
    return ((gradient - normed * projection) * inverse).astype(BF16)


def shards(
    image_residual_input,
    image_hidden_units,
    image_output_weight,
    text_residual_input,
    text_hidden_units,
    text_output_weight,
    log_logit_scale,
    pair_logit_bias,
):
    rows, width = image_residual_input.shape
    hidden = image_hidden_units.shape[1]
    n_run = lax.axis_size("run")
    n_place = lax.axis_size("place")
    n_dp = n_run * n_place
    n_replica = lax.axis_size("replica")
    n_tensor = lax.axis_size("tensor")
    run = lax.axis_index("run")
    place = lax.axis_index("place")
    replica = lax.axis_index("replica")
    tensor = lax.axis_index("tensor")
    own = rows // n_tensor
    members = n_replica * n_tensor
    columns = width // n_replica

    terms = jnp.concatenate(
        [
            dot(image_hidden_units, image_output_weight, ((1,), (0,)))
            .astype(BF16)
            .reshape(n_tensor, own, width),
            dot(text_hidden_units, text_output_weight, ((1,), (0,)))
            .astype(BF16)
            .reshape(n_tensor, own, width),
        ],
        axis=1,
    )
    summed = jnp.sum(exchange(terms, "tensor").astype(F32), axis=0)
    image_residual = lax.dynamic_slice_in_dim(image_residual_input, tensor * own, own, 0)
    text_residual = lax.dynamic_slice_in_dim(text_residual_input, tensor * own, own, 0)
    normed_text, inverse_text = normalize(text_residual, summed[own:])
    normed_image, inverse_image = normalize(image_residual, summed[:own])

    images = spread(normed_image.astype(BF16), PLANE)
    texts = gather_dp(normed_text.astype(BF16))
    texts, images = lax.optimization_barrier((texts, images))
    texts = texts.reshape(n_dp * own, width)
    images = images.reshape(members * own, width)

    scale = jnp.exp(log_logit_scale[0])
    logits = scale * dot(images, texts, ((1,), (1,))) + pair_logit_bias[0]
    image_index = jnp.arange(members * own, dtype=jnp.int32)
    position = jnp.arange(n_dp * own, dtype=jnp.int32)
    text_index = jnp.where(
        position // own == place * n_run + run,
        (replica * n_tensor + tensor) * own + position % own,
        -1,
    )
    label = jnp.where(image_index[:, None] == text_index[None, :], 1.0, -1.0).astype(F32)
    coefficients = (-label * jax.nn.sigmoid(-label * logits) * scale).astype(BF16)
    text_partial = dot(coefficients, images, ((0,), (0,))).astype(BF16)
    hidden_units = jnp.concatenate(
        [chunked(image_hidden_units, n_dp), chunked(text_hidden_units, n_dp)], axis=0
    )
    text_partial, coefficients, hidden_units = lax.optimization_barrier(
        (text_partial, coefficients, hidden_units)
    )
    text_grad = scatter_dp(text_partial.reshape(n_place, n_run, own, width))
    image_partial = dot(coefficients, texts, ((1,), (0,))).astype(BF16)
    image_parts = exchange(image_partial.reshape(members, own, width), PLANE)
    image_grad = jnp.sum(image_parts.astype(F32), axis=0)
    hidden_units = spread(hidden_units, "replica")
    text_grad, image_grad, hidden_units = lax.optimization_barrier(
        (text_grad, image_grad, hidden_units)
    )

    upstream_image = retract(normed_image, inverse_image, image_grad)
    upstream_text = retract(normed_text, inverse_text, text_grad)
    cut = jnp.concatenate(
        [
            upstream_image.reshape(own, n_replica, columns),
            upstream_text.reshape(own, n_replica, columns),
        ],
        axis=2,
    )
    cut = jnp.transpose(cut, (1, 0, 2))
    cut = jnp.broadcast_to(cut[:, None], (n_replica, n_tensor, own, 2 * columns))
    cut = exchange(cut.reshape(members, own, 2 * columns), PLANE)
    cut = cut.reshape(members * own, 2 * columns)
    slots = hidden_units.shape[1] // 2
    hidden_units = jnp.transpose(hidden_units, (1, 0, 2)).reshape(2 * slots, members * own)
    partial = dot(hidden_units, cut, ((1,), (0,)))
    partial = jnp.where(
        jnp.arange(2 * columns)[None, :] < columns, partial[:slots], partial[slots:]
    ).astype(BF16)
    partial = partial.reshape(n_place, n_run, slots // n_dp, 2 * columns)
    share = scatter_dp(partial).astype(BF16)
    total = gather_dp(share).reshape(n_dp, slots // n_dp, 2 * columns)
    total = total[:, : hidden // n_dp].astype(F32).reshape(hidden, 2 * columns)

    group = after(jnp.stack([upstream_image, upstream_text]), cut)
    group = lax.all_gather(group, "tensor", axis=1)
    hidden_grad_image = dot(
        group[0].reshape(rows, width), image_output_weight, ((1,), (1,))
    ).astype(BF16)
    hidden_grad_text = dot(
        group[1].reshape(rows, width), text_output_weight, ((1,), (1,))
    ).astype(BF16)

    return (hidden_grad_image, hidden_grad_text, total[:, :columns], total[:, columns:])


def solution(mesh):
    n_dp, n_replica, n_tensor = mesh.devices.shape
    n_run = math.isqrt(n_dp)
    mesh = Mesh(
        mesh.devices.reshape(n_run, n_dp // n_run, n_replica, n_tensor),
        ("run", "place", "replica", "tensor"),
    )
    rows = ("run", "place", "replica")
    in_specs = (
        P(rows, None),
        P(rows, "tensor"),
        P("tensor", None),
        P(rows, None),
        P(rows, "tensor"),
        P("tensor", None),
        P(),
        P(),
    )
    out_specs = (
        P(rows, "tensor"),
        P(rows, "tensor"),
        P("tensor", "replica"),
        P("tensor", "replica"),
    )
    return jax.shard_map(shards, mesh=mesh, in_specs=in_specs, out_specs=out_specs, check_vma=False)
```

```python
import jax
import jax.numpy as jnp
from jax import lax
from jax.sharding import PartitionSpec as P

F32 = jnp.float32
BF16 = jnp.bfloat16
PLANE = ("replica", "tensor")


def dot(a, b, contract):
    return lax.dot_general(a, b, (contract, ((), ())), preferred_element_type=F32)


def exchange(x, axis):
    return lax.all_to_all(x, axis, split_axis=0, concat_axis=0, tiled=True)


def spread(x, axis):
    size = lax.axis_size(axis)
    return exchange(jnp.broadcast_to(x[None], (size,) + x.shape), axis)


def after(x, *others):
    return lax.optimization_barrier((x,) + others)[0]


OFFSETS = (0, -4, -8, -12, -1, -5, -9, -13, 1, -3, -7, -11, 2, -2, -6, -10)


def shift(x, by):
    size = lax.axis_size("dp")
    return lax.ppermute(x, "dp", [(i, (i + by) % size) for i in range(size)])


def gather_dp(x):
    half = x.shape[0] // 16 * 8
    below = shift(x, 4)
    above = shift(x, -4)
    far = jnp.concatenate([shift(above[:half], -4), shift(below[half:], 4)], axis=0)
    quad = jnp.stack([x, below, far, above])
    return jnp.concatenate(
        [quad, shift(quad, 1), shift(quad, -1), shift(quad[0:2], -2), shift(quad[1:3], 2)],
        axis=0,
    )


def scatter_dp(x):
    half = x.shape[1] // 16 * 8
    one = shift(x[4:8], -1)
    two = shift(x[8:12], 1)
    three = shift(x[12:14], 2)
    four = shift(x[14:16], -2)
    quad = x[0:4].astype(F32) + one.astype(F32) + two.astype(F32)
    near = quad[0] + three[0].astype(F32)
    below = quad[1] + three[1].astype(F32) + four[0].astype(F32)
    far = (quad[2] + four[1].astype(F32)).astype(BF16)
    above = quad[3]
    above_half = shift(far[:half], 4).astype(F32)
    below_half = shift(far[half:], -4).astype(F32)
    above = jnp.concatenate([above[:half] + above_half, above[half:]], axis=0).astype(BF16)
    below = jnp.concatenate([below[:half], below[half:] + below_half], axis=0).astype(BF16)
    return near + shift(above, 4).astype(F32) + shift(below, -4).astype(F32)


def normalize(residual, summed):
    combined = residual.astype(F32) + summed
    inverse = lax.rsqrt(jnp.sum(combined * combined, axis=1, keepdims=True) + 1e-06)
    return (combined * inverse, inverse)


def retract(normed, inverse, gradient):
    projection = jnp.sum(normed * gradient, axis=1, keepdims=True)
    return ((gradient - normed * projection) * inverse).astype(BF16)


def shards(
    image_residual_input,
    image_hidden_units,
    image_output_weight,
    text_residual_input,
    text_hidden_units,
    text_output_weight,
    log_logit_scale,
    pair_logit_bias,
):
    rows, width = image_residual_input.shape
    n_dp = lax.axis_size("dp")
    n_replica = lax.axis_size("replica")
    n_tensor = lax.axis_size("tensor")
    replica = lax.axis_index("replica")
    tensor = lax.axis_index("tensor")
    own = rows // n_tensor
    members = n_replica * n_tensor
    columns = width // n_replica

    terms = jnp.concatenate(
        [
            dot(image_hidden_units, image_output_weight, ((1,), (0,)))
            .astype(BF16)
            .reshape(n_tensor, own, width),
            dot(text_hidden_units, text_output_weight, ((1,), (0,)))
            .astype(BF16)
            .reshape(n_tensor, own, width),
        ],
        axis=1,
    )
    summed = jnp.sum(exchange(terms, "tensor").astype(F32), axis=0)
    image_residual = lax.dynamic_slice_in_dim(image_residual_input, tensor * own, own, 0)
    text_residual = lax.dynamic_slice_in_dim(text_residual_input, tensor * own, own, 0)
    normed_text, inverse_text = normalize(text_residual, summed[own:])
    normed_image, inverse_image = normalize(image_residual, summed[:own])

    hidden_image, hidden_text = (
        lax.all_gather(after(units, summed), "replica", axis=0, tiled=True)
        for units in (image_hidden_units, text_hidden_units)
    )

    images = spread(normed_image.astype(BF16), PLANE)
    texts = gather_dp(normed_text.astype(BF16))
    texts, images = lax.optimization_barrier((texts, images))
    texts = texts.reshape(n_dp * own, width)
    images = images.reshape(members * own, width)

    scale = jnp.exp(log_logit_scale[0])
    logits = scale * dot(images, texts, ((1,), (1,))) + pair_logit_bias[0]
    image_index = jnp.arange(members * own, dtype=jnp.int32)
    position = jnp.arange(n_dp * own, dtype=jnp.int32)
    text_index = jnp.where(position < own, (replica * n_tensor + tensor) * own + position, -1)
    label = jnp.where(image_index[:, None] == text_index[None, :], 1.0, -1.0).astype(F32)
    coefficients = (-label * jax.nn.sigmoid(-label * logits) * scale).astype(BF16)
    text_partial = dot(coefficients, images, ((0,), (0,))).astype(BF16)
    image_partial = dot(after(coefficients, text_partial), texts, ((1,), (0,))).astype(BF16)

    text_grad = scatter_dp(text_partial.reshape(n_dp, own, width))
    image_parts = exchange(image_partial.reshape(members, own, width), PLANE)
    image_grad = jnp.sum(image_parts.astype(F32), axis=0)

    upstream_image = retract(normed_image, inverse_image, image_grad)
    upstream_text = retract(normed_text, inverse_text, text_grad)
    cut = jnp.concatenate(
        [
            upstream_image.reshape(own, n_replica, columns),
            upstream_text.reshape(own, n_replica, columns),
        ],
        axis=2,
    )
    cut = jnp.transpose(cut, (1, 0, 2))
    cut = jnp.broadcast_to(cut[:, None], (n_replica, n_tensor, own, 2 * columns))
    cut = exchange(cut.reshape(members, own, 2 * columns), PLANE)
    cut = cut.reshape(members * own, 2 * columns)
    group = lax.all_gather(jnp.stack([upstream_image, upstream_text]), "tensor", axis=1)
    hidden_grad_image = dot(
        group[0].reshape(rows, width), image_output_weight, ((1,), (1,))
    ).astype(BF16)
    hidden_grad_text = dot(
        group[1].reshape(rows, width), text_output_weight, ((1,), (1,))
    ).astype(BF16)

    partial = jnp.where(
        jnp.arange(2 * columns)[None, :] < columns,
        dot(hidden_image, cut, ((0,), (0,))),
        dot(hidden_text, cut, ((0,), (0,))),
    ).astype(BF16)
    partial, hidden_grad_image, hidden_grad_text = lax.optimization_barrier(
        (partial, hidden_grad_image, hidden_grad_text)
    )
    total = lax.psum(partial, "dp").astype(F32)
    return (hidden_grad_image, hidden_grad_text, total[:, :columns], total[:, columns:])


def solution(mesh):
    in_specs = (
        P(("dp", "replica"), None),
        P(("dp", "replica"), "tensor"),
        P("tensor", None),
        P(("dp", "replica"), None),
        P(("dp", "replica"), "tensor"),
        P("tensor", None),
        P(),
        P(),
    )
    out_specs = (
        P(("dp", "replica"), "tensor"),
        P(("dp", "replica"), "tensor"),
        P("tensor", "replica"),
        P("tensor", "replica"),
    )
    return jax.shard_map(shards, mesh=mesh, in_specs=in_specs, out_specs=out_specs, check_vma=False)
```

```python
import jax
import jax.numpy as jnp
from jax import lax
from jax.sharding import PartitionSpec as P

F32 = jnp.float32
BF16 = jnp.bfloat16
PLANE = ("replica", "tensor")


def dot(a, b, contract):
    return lax.dot_general(a, b, (contract, ((), ())), preferred_element_type=F32)


def exchange(x, axis):
    return lax.all_to_all(x, axis, split_axis=0, concat_axis=0, tiled=True)


def spread(x, axis):
    size = lax.axis_size(axis)
    return exchange(jnp.broadcast_to(x[None], (size,) + x.shape), axis)


def after(x, *others):
    return lax.optimization_barrier((x,) + others)[0]


OFFSETS = (0, -4, -8, -12, -1, -5, -9, -13, 1, -3, -7, -11, 2, -2, -6, -10)


def shift(x, by):
    size = lax.axis_size("dp")
    return lax.ppermute(x, "dp", [(i, (i + by) % size) for i in range(size)])


def gather_dp(x):
    half = x.shape[0] // 16 * 8
    below = shift(x, 4)
    above = shift(x, -4)
    far = jnp.concatenate([shift(above[:half], -4), shift(below[half:], 4)], axis=0)
    quad = jnp.stack([x, below, far, above])
    return jnp.concatenate(
        [quad, shift(quad, 1), shift(quad, -1), shift(quad[0:2], -2), shift(quad[1:3], 2)],
        axis=0,
    )


def scatter_dp(x):
    half = x.shape[1] // 16 * 8
    one = shift(x[4:8], -1)
    two = shift(x[8:12], 1)
    three = shift(x[12:14], 2)
    four = shift(x[14:16], -2)
    quad = x[0:4].astype(F32) + one.astype(F32) + two.astype(F32)
    near = quad[0] + three[0].astype(F32)
    below = quad[1] + three[1].astype(F32) + four[0].astype(F32)
    far = (quad[2] + four[1].astype(F32)).astype(BF16)
    above = quad[3]
    above_half = shift(far[:half], 4).astype(F32)
    below_half = shift(far[half:], -4).astype(F32)
    above = jnp.concatenate([above[:half] + above_half, above[half:]], axis=0).astype(BF16)
    below = jnp.concatenate([below[:half], below[half:] + below_half], axis=0).astype(BF16)
    return near + shift(above, 4).astype(F32) + shift(below, -4).astype(F32)


def chunked(hidden_units, size):
    rows, hidden = hidden_units.shape
    chunk = hidden // size
    slots = -(-chunk // 8) * 8
    x = hidden_units.T.reshape(size, chunk, rows)
    return jnp.pad(x, ((0, 0), (0, slots - chunk), (0, 0))).reshape(size * slots, rows).T


def normalize(residual, summed):
    combined = residual.astype(F32) + summed
    inverse = lax.rsqrt(jnp.sum(combined * combined, axis=1, keepdims=True) + 1e-06)
    return (combined * inverse, inverse)


def retract(normed, inverse, gradient):
    projection = jnp.sum(normed * gradient, axis=1, keepdims=True)
    return ((gradient - normed * projection) * inverse).astype(BF16)


def shards(
    image_residual_input,
    image_hidden_units,
    image_output_weight,
    text_residual_input,
    text_hidden_units,
    text_output_weight,
    log_logit_scale,
    pair_logit_bias,
):
    rows, width = image_residual_input.shape
    n_dp = lax.axis_size("dp")
    n_replica = lax.axis_size("replica")
    n_tensor = lax.axis_size("tensor")
    replica = lax.axis_index("replica")
    tensor = lax.axis_index("tensor")
    own = rows // n_tensor
    members = n_replica * n_tensor
    columns = width // n_replica

    terms = jnp.concatenate(
        [
            dot(image_hidden_units, image_output_weight, ((1,), (0,)))
            .astype(BF16)
            .reshape(n_tensor, own, width),
            dot(text_hidden_units, text_output_weight, ((1,), (0,)))
            .astype(BF16)
            .reshape(n_tensor, own, width),
        ],
        axis=1,
    )
    summed = jnp.sum(exchange(terms, "tensor").astype(F32), axis=0)
    image_residual = lax.dynamic_slice_in_dim(image_residual_input, tensor * own, own, 0)
    text_residual = lax.dynamic_slice_in_dim(text_residual_input, tensor * own, own, 0)
    normed_text, inverse_text = normalize(text_residual, summed[own:])
    normed_image, inverse_image = normalize(image_residual, summed[:own])

    hidden_image, hidden_text = (
        lax.all_gather(after(chunked(units, n_dp), summed), "replica", axis=0, tiled=True)
        for units in (image_hidden_units, text_hidden_units)
    )

    images = spread(normed_image.astype(BF16), PLANE)
    texts = gather_dp(normed_text.astype(BF16))
    texts, images = lax.optimization_barrier((texts, images))
    texts = texts.reshape(n_dp * own, width)
    images = images.reshape(members * own, width)

    scale = jnp.exp(log_logit_scale[0])
    logits = scale * dot(images, texts, ((1,), (1,))) + pair_logit_bias[0]
    image_index = jnp.arange(members * own, dtype=jnp.int32)
    position = jnp.arange(n_dp * own, dtype=jnp.int32)
    text_index = jnp.where(position < own, (replica * n_tensor + tensor) * own + position, -1)
    label = jnp.where(image_index[:, None] == text_index[None, :], 1.0, -1.0).astype(F32)
    coefficients = (-label * jax.nn.sigmoid(-label * logits) * scale).astype(BF16)
    image_partial = dot(coefficients, texts, ((1,), (0,))).astype(BF16)
    coefficients, image_partial = lax.optimization_barrier((coefficients, image_partial))
    image_parts = exchange(image_partial.reshape(members, own, width), PLANE)
    text_partial = dot(coefficients, images, ((0,), (0,))).astype(BF16)
    text_grad = scatter_dp(text_partial.reshape(n_dp, own, width))
    image_grad = jnp.sum(image_parts.astype(F32), axis=0)

    upstream_image = retract(normed_image, inverse_image, image_grad)
    upstream_text = retract(normed_text, inverse_text, text_grad)
    cut = jnp.concatenate(
        [
            upstream_image.reshape(own, n_replica, columns),
            upstream_text.reshape(own, n_replica, columns),
        ],
        axis=2,
    )
    cut = jnp.transpose(cut, (1, 0, 2))
    cut = jnp.broadcast_to(cut[:, None], (n_replica, n_tensor, own, 2 * columns))
    cut = exchange(cut.reshape(members, own, 2 * columns), PLANE)
    cut = cut.reshape(members * own, 2 * columns)
    group = after(jnp.stack([upstream_image, upstream_text]), cut)
    group = lax.all_gather(group, "tensor", axis=1)
    hidden_grad_image = dot(
        group[0].reshape(rows, width), image_output_weight, ((1,), (1,))
    ).astype(BF16)
    hidden_grad_text = dot(
        group[1].reshape(rows, width), text_output_weight, ((1,), (1,))
    ).astype(BF16)

    partial = jnp.where(
        jnp.arange(2 * columns)[None, :] < columns,
        dot(hidden_image, cut, ((0,), (0,))),
        dot(hidden_text, cut, ((0,), (0,))),
    ).astype(BF16)
    chunk = image_hidden_units.shape[1] // n_dp
    pieces = exchange(partial.reshape(n_dp, -1, 2 * columns), "dp")
    share = jnp.sum(pieces.astype(F32), axis=0).astype(BF16)
    total = lax.all_gather(share, "dp", axis=0)[:, :chunk].astype(F32)
    total = total.reshape(n_dp * chunk, 2 * columns)
    return (hidden_grad_image, hidden_grad_text, total[:, :columns], total[:, columns:])


def solution(mesh):
    in_specs = (
        P(("dp", "replica"), None),
        P(("dp", "replica"), "tensor"),
        P("tensor", None),
        P(("dp", "replica"), None),
        P(("dp", "replica"), "tensor"),
        P("tensor", None),
        P(),
        P(),
    )
    out_specs = (
        P(("dp", "replica"), "tensor"),
        P(("dp", "replica"), "tensor"),
        P("tensor", "replica"),
        P("tensor", "replica"),
    )
    return jax.shard_map(shards, mesh=mesh, in_specs=in_specs, out_specs=out_specs, check_vma=False)
```

```python
import math

import jax
import jax.numpy as jnp
from jax import lax
from jax.sharding import Mesh
from jax.sharding import PartitionSpec as P

F32 = jnp.float32
BF16 = jnp.bfloat16
PLANE = ("replica", "tensor")
DP = ("run", "place")
LANES = 128


def dot(a, b, contract):
    return lax.dot_general(a, b, (contract, ((), ())), preferred_element_type=F32)


def exchange(x, axis):
    return lax.all_to_all(x, axis, split_axis=0, concat_axis=0, tiled=True)


def spread(x, axis):
    size = lax.axis_size(axis)
    return exchange(jnp.broadcast_to(x[None], (size,) + x.shape), axis)


def after(x, *others):
    return lax.optimization_barrier((x,) + others)[0]


def shift(x, by):
    size = lax.axis_size(DP)
    return lax.ppermute(x, DP, [(i, (i + by) % size) for i in range(size)])


def gather_dp(x):
    quad = lax.all_gather(x, "run", axis=0)
    return jnp.concatenate(
        [quad, shift(quad, 1), shift(quad, -1), shift(quad[0:2], -2), shift(quad[2:4], 2)],
        axis=0,
    )


def scatter_dp(x):
    half = x.shape[1] // 16 * 8
    run = lax.axis_index("run")
    one = shift(x[4:8], -1)
    two = shift(x[8:12], 1)
    three = shift(x[12:14], 2)
    four = shift(x[14:16], -2)
    quad = x[0:4].astype(F32) + one.astype(F32) + two.astype(F32)
    quad = quad + jnp.concatenate([three, four], axis=0).astype(F32)
    near, above, far, below = (
        lax.dynamic_index_in_dim(quad, (run + k) % 4, 0, keepdims=False) for k in range(4)
    )
    far = far.astype(BF16)
    above_half = shift(far[:half], 4).astype(F32)
    below_half = shift(far[half:], -4).astype(F32)
    above = jnp.concatenate([above[:half] + above_half, above[half:]], axis=0).astype(BF16)
    below = jnp.concatenate([below[:half], below[half:] + below_half], axis=0).astype(BF16)
    return near + shift(above, 4).astype(F32) + shift(below, -4).astype(F32)


def normalize(residual, summed):
    combined = residual.astype(F32) + summed
    inverse = lax.rsqrt(jnp.sum(combined * combined, axis=1, keepdims=True) + 1e-06)
    return (combined * inverse, inverse)


def retract(normed, inverse, gradient):
    projection = jnp.sum(normed * gradient, axis=1, keepdims=True)
    return ((gradient - normed * projection) * inverse).astype(BF16)


def shards(
    image_residual_input,
    image_hidden_units,
    image_output_weight,
    text_residual_input,
    text_hidden_units,
    text_output_weight,
    log_logit_scale,
    pair_logit_bias,
):
    rows, width = image_residual_input.shape
    n_dp = lax.axis_size(DP)
    n_replica = lax.axis_size("replica")
    n_tensor = lax.axis_size("tensor")
    replica = lax.axis_index("replica")
    tensor = lax.axis_index("tensor")
    own = rows // n_tensor
    members = n_replica * n_tensor
    columns = width // n_replica

    terms = jnp.concatenate(
        [
            dot(image_hidden_units, image_output_weight, ((1,), (0,)))
            .astype(BF16)
            .reshape(n_tensor, own, width),
            dot(text_hidden_units, text_output_weight, ((1,), (0,)))
            .astype(BF16)
            .reshape(n_tensor, own, width),
        ],
        axis=1,
    )
    summed = jnp.sum(exchange(terms, "tensor").astype(F32), axis=0)
    image_residual = lax.dynamic_slice_in_dim(image_residual_input, tensor * own, own, 0)
    text_residual = lax.dynamic_slice_in_dim(text_residual_input, tensor * own, own, 0)
    normed_text, inverse_text = normalize(text_residual, summed[own:])
    normed_image, inverse_image = normalize(image_residual, summed[:own])

    hidden_image, hidden_text = (
        lax.all_gather(after(units, summed), "replica", axis=0, tiled=True)
        for units in (image_hidden_units, text_hidden_units)
    )

    images = spread(normed_image.astype(BF16), PLANE)
    texts = gather_dp(normed_text.astype(BF16))
    texts, images = lax.optimization_barrier((texts, images))
    texts = texts.reshape(n_dp * own, width)
    images = images.reshape(members * own, width)

    scale = jnp.exp(log_logit_scale[0])
    logits = scale * dot(images, texts, ((1,), (1,))) + pair_logit_bias[0]
    image_index = jnp.arange(members * own, dtype=jnp.int32)
    position = jnp.arange(n_dp * own, dtype=jnp.int32)
    text_index = jnp.where(
        position // own == lax.axis_index("run"),
        (replica * n_tensor + tensor) * own + position % own,
        -1,
    )
    label = jnp.where(image_index[:, None] == text_index[None, :], 1.0, -1.0).astype(F32)
    coefficients = (-label * jax.nn.sigmoid(-label * logits) * scale).astype(BF16)
    image_partial = dot(coefficients, texts, ((1,), (0,))).astype(BF16)
    coefficients, image_partial = lax.optimization_barrier((coefficients, image_partial))
    image_parts = exchange(image_partial.reshape(members, own, width), PLANE)
    text_partial = dot(coefficients, images, ((0,), (0,))).astype(BF16)
    text_grad = scatter_dp(text_partial.reshape(n_dp, own, width))
    image_grad = jnp.sum(image_parts.astype(F32), axis=0)

    upstream_image = retract(normed_image, inverse_image, image_grad)
    upstream_text = retract(normed_text, inverse_text, text_grad)
    cut = jnp.concatenate(
        [
            upstream_image.reshape(own, n_replica, columns),
            upstream_text.reshape(own, n_replica, columns),
        ],
        axis=2,
    )
    cut = jnp.transpose(cut, (1, 0, 2))
    cut = jnp.broadcast_to(cut[:, None], (n_replica, n_tensor, own, 2 * columns))
    cut = exchange(cut.reshape(members, own, 2 * columns), PLANE)
    cut = cut.reshape(members * own, 2 * columns)
    group = after(jnp.stack([upstream_image, upstream_text]), cut)
    group = lax.all_gather(group, "tensor", axis=1)
    hidden_grad_image = dot(
        group[0].reshape(rows, width), image_output_weight, ((1,), (1,))
    ).astype(BF16)
    hidden_grad_text = dot(
        group[1].reshape(rows, width), text_output_weight, ((1,), (1,))
    ).astype(BF16)

    hidden = image_hidden_units.shape[1]
    side = lax.axis_size("run")
    partial = jnp.concatenate(
        [
            dot(cut, hidden_image, ((0,), (0,)))[:columns],
            dot(cut, hidden_text, ((0,), (0,)))[columns:],
        ],
        axis=0,
    ).astype(BF16)
    pieces = exchange(pack(partial, side), DP)
    share = jnp.sum(pieces.astype(F32), axis=0).astype(BF16)
    total = unpack(spread(share, DP), side, hidden).astype(F32)
    return (hidden_grad_image, hidden_grad_text, total[:columns].T, total[columns:].T)


def pack(x, side):
    high = x.shape[0] // side
    low = high // (side - 1)
    whole = x.shape[1] // LANES * LANES
    left = x.shape[1] - whole
    blocks = [
        x[:, k * LANES : (k + 1) * LANES].reshape(side, high, LANES) for k in range(side)
    ]
    rest = jnp.pad(x[:, whole:], ((0, 0), (0, LANES - left))).reshape(side, high, LANES)
    rests = [rest[:, k * low : (k + 1) * low] for k in range(side - 1)]
    rests.append(jnp.zeros_like(rests[0]))
    return jnp.concatenate(
        [jnp.concatenate(blocks, axis=0), jnp.concatenate(rests, axis=0)], axis=1
    )


def unpack(x, side, lanes):
    low = x.shape[1] // side
    high = x.shape[1] - low
    blocks = [
        x[k * side : (k + 1) * side, :high].reshape(side * high, LANES) for k in range(side)
    ]
    rest = [x[k * side : (k + 1) * side, high:] for k in range(side - 1)]
    rest = jnp.concatenate(rest, axis=1).reshape(side * high, LANES)
    return jnp.concatenate(blocks + [rest[:, : lanes - side * LANES]], axis=1)


def solution(mesh):
    n_dp, n_replica, n_tensor = mesh.devices.shape
    n_run = math.isqrt(n_dp)
    mesh = Mesh(
        mesh.devices.reshape(n_run, n_dp // n_run, n_replica, n_tensor),
        ("run", "place", "replica", "tensor"),
    )
    rows = ("run", "place", "replica")
    in_specs = (
        P(rows, None),
        P(rows, "tensor"),
        P("tensor", None),
        P(rows, None),
        P(rows, "tensor"),
        P("tensor", None),
        P(),
        P(),
    )
    out_specs = (
        P(rows, "tensor"),
        P(rows, "tensor"),
        P("tensor", "replica"),
        P("tensor", "replica"),
    )
    return jax.shard_map(shards, mesh=mesh, in_specs=in_specs, out_specs=out_specs, check_vma=False)
```

```python
import math

import jax
import jax.numpy as jnp
from jax import lax
from jax.sharding import Mesh
from jax.sharding import PartitionSpec as P

F32 = jnp.float32
BF16 = jnp.bfloat16
PLANE = ("replica", "tensor")
DP = ("run", "place")
LANES = 128


def dot(a, b, contract):
    return lax.dot_general(a, b, (contract, ((), ())), preferred_element_type=F32)


def exchange(x, axis):
    return lax.all_to_all(x, axis, split_axis=0, concat_axis=0, tiled=True)


def spread(x, axis):
    size = lax.axis_size(axis)
    return exchange(jnp.broadcast_to(x[None], (size,) + x.shape), axis)


def after(x, *others):
    return lax.optimization_barrier((x,) + others)[0]


def shift(x, by):
    size = lax.axis_size(DP)
    return lax.ppermute(x, DP, [(i, (i + by) % size) for i in range(size)])


def gather_dp(x):
    quad = lax.all_gather(x, "run", axis=0)
    return jnp.concatenate(
        [quad, shift(quad, 1), shift(quad, -1), shift(quad[0:2], -2), shift(quad[2:4], 2)],
        axis=0,
    )


def scatter_dp(x, meanwhile):
    half = x.shape[1] // 16 * 8
    run = lax.axis_index("run")
    one = shift(x[4:8], -1)
    two = shift(x[8:12], 1)
    three = shift(x[12:14], 2)
    four = shift(x[14:16], -2)
    quad = x[0:4].astype(F32) + one.astype(F32) + two.astype(F32)
    quad = quad + jnp.concatenate([three, four], axis=0).astype(F32)
    near, above, far, below = (
        lax.dynamic_index_in_dim(quad, (run + k) % 4, 0, keepdims=False) for k in range(4)
    )
    far = far.astype(BF16)
    above_half = shift(far[:half], 4).astype(F32)
    below_half = shift(far[half:], -4).astype(F32)
    above = jnp.concatenate([above[:half] + above_half, above[half:]], axis=0).astype(BF16)
    below = jnp.concatenate([below[:half], below[half:] + below_half], axis=0).astype(BF16)
    above, below, meanwhile = lax.optimization_barrier((above, below, meanwhile))
    total = near + shift(above, 4).astype(F32) + shift(below, -4).astype(F32)
    return (total, meanwhile)


def normalize(residual, summed):
    combined = residual.astype(F32) + summed
    inverse = lax.rsqrt(jnp.sum(combined * combined, axis=1, keepdims=True) + 1e-06)
    return (combined * inverse, inverse)


def retract(normed, inverse, gradient):
    projection = jnp.sum(normed * gradient, axis=1, keepdims=True)
    return ((gradient - normed * projection) * inverse).astype(BF16)


def shards(
    image_residual_input,
    image_hidden_units,
    image_output_weight,
    text_residual_input,
    text_hidden_units,
    text_output_weight,
    log_logit_scale,
    pair_logit_bias,
):
    rows, width = image_residual_input.shape
    n_dp = lax.axis_size(DP)
    n_replica = lax.axis_size("replica")
    n_tensor = lax.axis_size("tensor")
    replica = lax.axis_index("replica")
    tensor = lax.axis_index("tensor")
    own = rows // n_tensor
    members = n_replica * n_tensor
    columns = width // n_replica

    terms = jnp.concatenate(
        [
            dot(image_hidden_units, image_output_weight, ((1,), (0,)))
            .astype(BF16)
            .reshape(n_tensor, own, width),
            dot(text_hidden_units, text_output_weight, ((1,), (0,)))
            .astype(BF16)
            .reshape(n_tensor, own, width),
        ],
        axis=1,
    )
    summed = jnp.sum(exchange(terms, "tensor").astype(F32), axis=0)
    image_residual = lax.dynamic_slice_in_dim(image_residual_input, tensor * own, own, 0)
    text_residual = lax.dynamic_slice_in_dim(text_residual_input, tensor * own, own, 0)
    normed_text, inverse_text = normalize(text_residual, summed[own:])
    normed_image, inverse_image = normalize(image_residual, summed[:own])

    hidden_image, hidden_text = (
        lax.all_gather(after(units, summed), "replica", axis=0, tiled=True)
        for units in (image_hidden_units, text_hidden_units)
    )

    images = spread(normed_image.astype(BF16), PLANE)
    texts = gather_dp(normed_text.astype(BF16))
    texts, images = lax.optimization_barrier((texts, images))
    texts = texts.reshape(n_dp * own, width)
    images = images.reshape(members * own, width)

    scale = jnp.exp(log_logit_scale[0])
    logits = scale * dot(images, texts, ((1,), (1,))) + pair_logit_bias[0]
    image_index = jnp.arange(members * own, dtype=jnp.int32)
    position = jnp.arange(n_dp * own, dtype=jnp.int32)
    text_index = jnp.where(
        position // own == lax.axis_index("run"),
        (replica * n_tensor + tensor) * own + position % own,
        -1,
    )
    label = jnp.where(image_index[:, None] == text_index[None, :], 1.0, -1.0).astype(F32)
    coefficients = (-label * jax.nn.sigmoid(-label * logits) * scale).astype(BF16)
    image_partial = dot(coefficients, texts, ((1,), (0,))).astype(BF16)
    coefficients, image_partial = lax.optimization_barrier((coefficients, image_partial))
    image_parts = exchange(image_partial.reshape(members, own, width), PLANE)
    text_partial = dot(coefficients, images, ((0,), (0,))).astype(BF16)
    text_partial, hidden_text = lax.optimization_barrier((text_partial, hidden_text))
    text_grad, image_parts = scatter_dp(text_partial.reshape(n_dp, own, width), image_parts)
    image_grad = jnp.sum(image_parts.astype(F32), axis=0)
    image_grad, hidden_image = lax.optimization_barrier((image_grad, hidden_image))

    upstream_image = retract(normed_image, inverse_image, image_grad)
    upstream_text = retract(normed_text, inverse_text, text_grad)
    cut = jnp.concatenate(
        [
            upstream_image.reshape(own, n_replica, columns),
            upstream_text.reshape(own, n_replica, columns),
        ],
        axis=2,
    )
    cut = jnp.transpose(cut, (1, 0, 2))
    cut = jnp.broadcast_to(cut[:, None], (n_replica, n_tensor, own, 2 * columns))
    cut = exchange(cut.reshape(members, own, 2 * columns), PLANE)
    cut = cut.reshape(members * own, 2 * columns)
    group = after(jnp.stack([upstream_image, upstream_text]), cut)
    group = lax.all_gather(group, "tensor", axis=1)
    hidden_grad_image = dot(
        group[0].reshape(rows, width), image_output_weight, ((1,), (1,))
    ).astype(BF16)
    hidden_grad_text = dot(
        group[1].reshape(rows, width), text_output_weight, ((1,), (1,))
    ).astype(BF16)

    hidden = image_hidden_units.shape[1]
    side = lax.axis_size("run")
    partial = jnp.concatenate(
        [
            dot(cut, hidden_image, ((0,), (0,)))[:columns],
            dot(cut, hidden_text, ((0,), (0,)))[columns:],
        ],
        axis=0,
    ).astype(BF16)
    pieces = exchange(pack(partial, side), DP)
    share = jnp.sum(pieces.astype(F32), axis=0).astype(BF16)
    total = unpack(spread(share, DP), side, hidden).astype(F32)
    return (hidden_grad_image, hidden_grad_text, total[:columns].T, total[columns:].T)


def pack(x, side):
    size = side * side
    high = x.shape[0] // side
    whole = side * LANES
    blocks = [
        x[:, k * LANES : (k + 1) * LANES].reshape(side, high, LANES) for k in range(side)
    ]
    rest = [x[k * high : (k + 1) * high, whole:] for k in range(side)]
    rest = jnp.concatenate(rest, axis=1).reshape(high // 8, 8, LANES)
    rest = jnp.pad(rest, ((0, size - high // 8), (0, 0), (0, 0)))
    return jnp.concatenate([jnp.concatenate(blocks, axis=0), rest], axis=1)


def unpack(x, side, lanes):
    high = x.shape[1] - 8
    left = lanes - side * LANES
    blocks = [
        x[k * side : (k + 1) * side, :high].reshape(side * high, LANES) for k in range(side)
    ]
    rest = x[: high // 8, high:].reshape(high, LANES)
    rest = [rest[:, k * left : (k + 1) * left] for k in range(side)]
    return jnp.concatenate(blocks + [jnp.concatenate(rest, axis=0)], axis=1)


def solution(mesh):
    n_dp, n_replica, n_tensor = mesh.devices.shape
    n_run = math.isqrt(n_dp)
    mesh = Mesh(
        mesh.devices.reshape(n_run, n_dp // n_run, n_replica, n_tensor),
        ("run", "place", "replica", "tensor"),
    )
    rows = ("run", "place", "replica")
    in_specs = (
        P(rows, None),
        P(rows, "tensor"),
        P("tensor", None),
        P(rows, None),
        P(rows, "tensor"),
        P("tensor", None),
        P(),
        P(),
    )
    out_specs = (
        P(rows, "tensor"),
        P(rows, "tensor"),
        P("tensor", "replica"),
        P("tensor", "replica"),
    )
    return jax.shard_map(shards, mesh=mesh, in_specs=in_specs, out_specs=out_specs, check_vma=False)
```

```python
import math

import jax
import jax.numpy as jnp
from jax import lax
from jax.sharding import Mesh
from jax.sharding import PartitionSpec as P

F32 = jnp.float32
BF16 = jnp.bfloat16
PLANE = ("replica", "tensor")
DP = ("run", "place")
LANES = 128


def dot(a, b, contract):
    return lax.dot_general(a, b, (contract, ((), ())), preferred_element_type=F32)


def exchange(x, axis):
    return lax.all_to_all(x, axis, split_axis=0, concat_axis=0, tiled=True)


def spread(x, axis):
    size = lax.axis_size(axis)
    return exchange(jnp.broadcast_to(x[None], (size,) + x.shape), axis)


def after(x, *others):
    return lax.optimization_barrier((x,) + others)[0]


def shift(x, by):
    size = lax.axis_size(DP)
    return lax.ppermute(x, DP, [(i, (i + by) % size) for i in range(size)])


def gather_dp(x):
    quad = lax.all_gather(x, "run", axis=0)
    return jnp.concatenate(
        [quad, shift(quad, 1), shift(quad, -1), shift(quad[0:2], -2), shift(quad[2:4], 2)],
        axis=0,
    )


def scatter_dp(x):
    half = x.shape[1] // 16 * 8
    run = lax.axis_index("run")
    one = shift(x[4:8], -1)
    two = shift(x[8:12], 1)
    three = shift(x[12:14], 2)
    four = shift(x[14:16], -2)
    quad = x[0:4].astype(F32) + one.astype(F32) + two.astype(F32)
    quad = quad + jnp.concatenate([three, four], axis=0).astype(F32)
    near, above, far, below = (
        lax.dynamic_index_in_dim(quad, (run + k) % 4, 0, keepdims=False) for k in range(4)
    )
    far = far.astype(BF16)
    above_half = shift(far[:half], 4).astype(F32)
    below_half = shift(far[half:], -4).astype(F32)
    above = jnp.concatenate([above[:half] + above_half, above[half:]], axis=0).astype(BF16)
    below = jnp.concatenate([below[:half], below[half:] + below_half], axis=0).astype(BF16)
    return near + shift(above, 4).astype(F32) + shift(below, -4).astype(F32)


def normalize(residual, summed):
    combined = residual.astype(F32) + summed
    inverse = lax.rsqrt(jnp.sum(combined * combined, axis=1, keepdims=True) + 1e-06)
    return (combined * inverse, inverse)


def retract(normed, inverse, gradient):
    projection = jnp.sum(normed * gradient, axis=1, keepdims=True)
    return ((gradient - normed * projection) * inverse).astype(BF16)


def shards(
    image_residual_input,
    image_hidden_units,
    image_output_weight,
    text_residual_input,
    text_hidden_units,
    text_output_weight,
    log_logit_scale,
    pair_logit_bias,
):
    rows, width = image_residual_input.shape
    n_dp = lax.axis_size(DP)
    n_replica = lax.axis_size("replica")
    n_tensor = lax.axis_size("tensor")
    replica = lax.axis_index("replica")
    tensor = lax.axis_index("tensor")
    own = rows // n_tensor
    members = n_replica * n_tensor
    columns = width // n_replica

    terms = jnp.concatenate(
        [
            dot(image_hidden_units, image_output_weight, ((1,), (0,)))
            .astype(BF16)
            .reshape(n_tensor, own, width),
            dot(text_hidden_units, text_output_weight, ((1,), (0,)))
            .astype(BF16)
            .reshape(n_tensor, own, width),
        ],
        axis=1,
    )
    summed = jnp.sum(exchange(terms, "tensor").astype(F32), axis=0)
    image_residual = lax.dynamic_slice_in_dim(image_residual_input, tensor * own, own, 0)
    text_residual = lax.dynamic_slice_in_dim(text_residual_input, tensor * own, own, 0)
    normed_text, inverse_text = normalize(text_residual, summed[own:])
    normed_image, inverse_image = normalize(image_residual, summed[:own])

    hidden_image, hidden_text = (
        lax.all_gather(after(units, summed), "replica", axis=0, tiled=True)
        for units in (image_hidden_units, text_hidden_units)
    )

    images = spread(normed_image.astype(BF16), PLANE)
    texts = gather_dp(normed_text.astype(BF16))
    texts, images = lax.optimization_barrier((texts, images))
    texts = texts.reshape(n_dp * own, width)
    images = images.reshape(members * own, width)

    scale = jnp.exp(log_logit_scale[0])
    logits = scale * dot(images, texts, ((1,), (1,))) + pair_logit_bias[0]
    image_index = jnp.arange(members * own, dtype=jnp.int32)
    position = jnp.arange(n_dp * own, dtype=jnp.int32)
    text_index = jnp.where(
        position // own == lax.axis_index("run"),
        (replica * n_tensor + tensor) * own + position % own,
        -1,
    )
    label = jnp.where(image_index[:, None] == text_index[None, :], 1.0, -1.0).astype(F32)
    coefficients = (-label * jax.nn.sigmoid(-label * logits) * scale).astype(BF16)
    image_partial = dot(coefficients, texts, ((1,), (0,))).astype(BF16)
    coefficients, image_partial = lax.optimization_barrier((coefficients, image_partial))
    image_parts = exchange(image_partial.reshape(members, own, width), PLANE)
    text_partial = dot(coefficients, images, ((0,), (0,))).astype(BF16)
    text_grad = scatter_dp(text_partial.reshape(n_dp, own, width))
    image_grad = jnp.sum(image_parts.astype(F32), axis=0)

    upstream_image = retract(normed_image, inverse_image, image_grad)
    upstream_text = retract(normed_text, inverse_text, text_grad)
    cut = jnp.concatenate(
        [
            upstream_image.reshape(own, n_replica, columns),
            upstream_text.reshape(own, n_replica, columns),
        ],
        axis=2,
    )
    cut = exchange(jnp.transpose(cut, (1, 0, 2)), "replica")
    cut = lax.all_gather(cut, "tensor", axis=1).reshape(members * own, 2 * columns)
    group = after(jnp.stack([upstream_image, upstream_text]), cut)
    group = lax.all_gather(group, "tensor", axis=1)
    hidden_grad_image = dot(
        group[0].reshape(rows, width), image_output_weight, ((1,), (1,))
    ).astype(BF16)
    hidden_grad_text = dot(
        group[1].reshape(rows, width), text_output_weight, ((1,), (1,))
    ).astype(BF16)

    hidden = image_hidden_units.shape[1]
    side = lax.axis_size("run")
    partial = jnp.concatenate(
        [
            dot(cut, hidden_image, ((0,), (0,)))[:columns],
            dot(cut, hidden_text, ((0,), (0,)))[columns:],
        ],
        axis=0,
    ).astype(BF16)
    pieces = exchange(pack(partial, side), DP)
    share = jnp.sum(pieces.astype(F32), axis=0).astype(BF16)
    total = unpack(spread(share, DP), side, hidden).astype(F32)
    return (hidden_grad_image, hidden_grad_text, total[:columns].T, total[columns:].T)


def pack(x, side):
    size = side * side
    high = x.shape[0] // side
    whole = side * LANES
    blocks = [
        x[:, k * LANES : (k + 1) * LANES].reshape(side, high, LANES) for k in range(side)
    ]
    rest = [x[k * high : (k + 1) * high, whole:] for k in range(side)]
    rest = jnp.concatenate(rest, axis=1).reshape(high // 8, 8, LANES)
    rest = jnp.pad(rest, ((0, size - high // 8), (0, 0), (0, 0)))
    return jnp.concatenate([jnp.concatenate(blocks, axis=0), rest], axis=1)


def unpack(x, side, lanes):
    high = x.shape[1] - 8
    left = lanes - side * LANES
    blocks = [
        x[k * side : (k + 1) * side, :high].reshape(side * high, LANES) for k in range(side)
    ]
    rest = x[: high // 8, high:].reshape(high, LANES)
    rest = [rest[:, k * left : (k + 1) * left] for k in range(side)]
    return jnp.concatenate(blocks + [jnp.concatenate(rest, axis=0)], axis=1)


def solution(mesh):
    n_dp, n_replica, n_tensor = mesh.devices.shape
    n_run = math.isqrt(n_dp)
    mesh = Mesh(
        mesh.devices.reshape(n_run, n_dp // n_run, n_replica, n_tensor),
        ("run", "place", "replica", "tensor"),
    )
    rows = ("run", "place", "replica")
    in_specs = (
        P(rows, None),
        P(rows, "tensor"),
        P("tensor", None),
        P(rows, None),
        P(rows, "tensor"),
        P("tensor", None),
        P(),
        P(),
    )
    out_specs = (
        P(rows, "tensor"),
        P(rows, "tensor"),
        P("tensor", "replica"),
        P("tensor", "replica"),
    )
    return jax.shard_map(shards, mesh=mesh, in_specs=in_specs, out_specs=out_specs, check_vma=False)
```

```python
import math

import jax
import jax.numpy as jnp
from jax import lax
from jax.sharding import Mesh
from jax.sharding import PartitionSpec as P

F32 = jnp.float32
BF16 = jnp.bfloat16
PLANE = ("replica", "tensor")
DP = ("run", "place")
LANES = 128


def dot(a, b, contract):
    return lax.dot_general(a, b, (contract, ((), ())), preferred_element_type=F32)


def exchange(x, axis):
    return lax.all_to_all(x, axis, split_axis=0, concat_axis=0, tiled=True)


def spread(x, axis):
    size = lax.axis_size(axis)
    return exchange(jnp.broadcast_to(x[None], (size,) + x.shape), axis)


def after(x, *others):
    return lax.optimization_barrier((x,) + others)[0]


def shift(x, by):
    size = lax.axis_size(DP)
    return lax.ppermute(x, DP, [(i, (i + by) % size) for i in range(size)])


def gather_dp(x):
    quad = lax.all_gather(x, "run", axis=0)
    return (
        jnp.concatenate([quad, shift(quad, 1), shift(quad, -1)], axis=0),
        jnp.concatenate([shift(quad[0:2], -2), shift(quad[2:4], 2)], axis=0),
    )


def scatter_dp(x, y):
    half = x.shape[1] // 16 * 8
    run = lax.axis_index("run")
    one = shift(x[4:8], -1)
    two = shift(x[8:12], 1)
    three = shift(y[0:2], 2)
    four = shift(y[2:4], -2)
    quad = x[0:4].astype(F32) + one.astype(F32) + two.astype(F32)
    quad = quad + jnp.concatenate([three, four], axis=0).astype(F32)
    near, above, far, below = (
        lax.dynamic_index_in_dim(quad, (run + k) % 4, 0, keepdims=False) for k in range(4)
    )
    far = far.astype(BF16)
    above_half = shift(far[:half], 4).astype(F32)
    below_half = shift(far[half:], -4).astype(F32)
    above = jnp.concatenate([above[:half] + above_half, above[half:]], axis=0).astype(BF16)
    below = jnp.concatenate([below[:half], below[half:] + below_half], axis=0).astype(BF16)
    return near + shift(above, 4).astype(F32) + shift(below, -4).astype(F32)


def normalize(residual, summed):
    combined = residual.astype(F32) + summed
    inverse = lax.rsqrt(jnp.sum(combined * combined, axis=1, keepdims=True) + 1e-06)
    return (combined * inverse, inverse)


def retract(normed, inverse, gradient):
    projection = jnp.sum(normed * gradient, axis=1, keepdims=True)
    return ((gradient - normed * projection) * inverse).astype(BF16)


def shards(
    image_residual_input,
    image_hidden_units,
    image_output_weight,
    text_residual_input,
    text_hidden_units,
    text_output_weight,
    log_logit_scale,
    pair_logit_bias,
):
    rows, width = image_residual_input.shape
    n_dp = lax.axis_size(DP)
    n_replica = lax.axis_size("replica")
    n_tensor = lax.axis_size("tensor")
    replica = lax.axis_index("replica")
    tensor = lax.axis_index("tensor")
    own = rows // n_tensor
    members = n_replica * n_tensor
    columns = width // n_replica

    terms = jnp.concatenate(
        [
            dot(image_hidden_units, image_output_weight, ((1,), (0,)))
            .astype(BF16)
            .reshape(n_tensor, own, width),
            dot(text_hidden_units, text_output_weight, ((1,), (0,)))
            .astype(BF16)
            .reshape(n_tensor, own, width),
        ],
        axis=1,
    )
    summed = jnp.sum(exchange(terms, "tensor").astype(F32), axis=0)
    image_residual = lax.dynamic_slice_in_dim(image_residual_input, tensor * own, own, 0)
    text_residual = lax.dynamic_slice_in_dim(text_residual_input, tensor * own, own, 0)
    normed_text, inverse_text = normalize(text_residual, summed[own:])
    normed_image, inverse_image = normalize(image_residual, summed[:own])

    hidden_image, hidden_text = (
        lax.all_gather(after(units, summed), "replica", axis=0, tiled=True)
        for units in (image_hidden_units, text_hidden_units)
    )

    images = spread(normed_image.astype(BF16), PLANE)
    near, next_near = gather_dp(normed_text.astype(BF16))
    near = near.reshape(-1, width)
    next_near = next_near.reshape(-1, width)
    images = images.reshape(members * own, width)

    scale = jnp.exp(log_logit_scale[0])

    image_index = jnp.arange(members * own, dtype=jnp.int32)
    position = jnp.arange(near.shape[0], dtype=jnp.int32)
    text_index = jnp.where(
        position // own == lax.axis_index("run"),
        (replica * n_tensor + tensor) * own + position % own,
        -1,
    )
    logits = scale * dot(images, near, ((1,), (1,))) + pair_logit_bias[0]
    label = jnp.where(image_index[:, None] == text_index[None, :], 1.0, -1.0).astype(F32)
    near_pairs = (-label * jax.nn.sigmoid(-label * logits) * scale).astype(BF16)
    logits = scale * dot(images, next_near, ((1,), (1,))) + pair_logit_bias[0]
    next_pairs = (jax.nn.sigmoid(logits) * scale).astype(BF16)
    image_partial = dot(
        jnp.concatenate([near_pairs, next_pairs], axis=1),
        jnp.concatenate([near, next_near], axis=0),
        ((1,), (0,)),
    ).astype(BF16)
    near_pairs, next_pairs, image_partial = lax.optimization_barrier(
        (near_pairs, next_pairs, image_partial)
    )
    image_parts = exchange(image_partial.reshape(members, own, width), PLANE)
    text_grad = scatter_dp(
        dot(near_pairs, images, ((0,), (0,))).astype(BF16).reshape(-1, own, width),
        dot(next_pairs, images, ((0,), (0,))).astype(BF16).reshape(-1, own, width),
    )
    image_grad = jnp.sum(image_parts.astype(F32), axis=0)

    upstream_image = retract(normed_image, inverse_image, image_grad)
    upstream_text = retract(normed_text, inverse_text, text_grad)
    cut = jnp.concatenate(
        [
            upstream_image.reshape(own, n_replica, columns),
            upstream_text.reshape(own, n_replica, columns),
        ],
        axis=2,
    )
    cut = jnp.transpose(cut, (1, 0, 2))
    cut = jnp.broadcast_to(cut[:, None], (n_replica, n_tensor, own, 2 * columns))
    cut = exchange(cut.reshape(members, own, 2 * columns), PLANE)
    cut = cut.reshape(members * own, 2 * columns)
    group = after(jnp.stack([upstream_image, upstream_text]), cut)
    group = lax.all_gather(group, "tensor", axis=1)
    hidden_grad_image = dot(
        group[0].reshape(rows, width), image_output_weight, ((1,), (1,))
    ).astype(BF16)
    hidden_grad_text = dot(
        group[1].reshape(rows, width), text_output_weight, ((1,), (1,))
    ).astype(BF16)

    hidden = image_hidden_units.shape[1]
    side = lax.axis_size("run")
    partial = jnp.concatenate(
        [
            dot(cut, hidden_image, ((0,), (0,)))[:columns],
            dot(cut, hidden_text, ((0,), (0,)))[columns:],
        ],
        axis=0,
    ).astype(BF16)
    pieces = exchange(pack(partial, side), DP)
    share = jnp.sum(pieces.astype(F32), axis=0).astype(BF16)
    total = unpack(spread(share, DP), side, hidden).astype(F32)
    return (hidden_grad_image, hidden_grad_text, total[:columns].T, total[columns:].T)


def pack(x, side):
    size = side * side
    high = x.shape[0] // side
    whole = side * LANES
    blocks = [
        x[:, k * LANES : (k + 1) * LANES].reshape(side, high, LANES) for k in range(side)
    ]
    rest = [x[k * high : (k + 1) * high, whole:] for k in range(side)]
    rest = jnp.concatenate(rest, axis=1).reshape(high // 8, 8, LANES)
    rest = jnp.pad(rest, ((0, size - high // 8), (0, 0), (0, 0)))
    return jnp.concatenate([jnp.concatenate(blocks, axis=0), rest], axis=1)


def unpack(x, side, lanes):
    high = x.shape[1] - 8
    left = lanes - side * LANES
    blocks = [
        x[k * side : (k + 1) * side, :high].reshape(side * high, LANES) for k in range(side)
    ]
    rest = x[: high // 8, high:].reshape(high, LANES)
    rest = [rest[:, k * left : (k + 1) * left] for k in range(side)]
    return jnp.concatenate(blocks + [jnp.concatenate(rest, axis=0)], axis=1)


def solution(mesh):
    n_dp, n_replica, n_tensor = mesh.devices.shape
    n_run = math.isqrt(n_dp)
    mesh = Mesh(
        mesh.devices.reshape(n_run, n_dp // n_run, n_replica, n_tensor),
        ("run", "place", "replica", "tensor"),
    )
    rows = ("run", "place", "replica")
    in_specs = (
        P(rows, None),
        P(rows, "tensor"),
        P("tensor", None),
        P(rows, None),
        P(rows, "tensor"),
        P("tensor", None),
        P(),
        P(),
    )
    out_specs = (
        P(rows, "tensor"),
        P(rows, "tensor"),
        P("tensor", "replica"),
        P("tensor", "replica"),
    )
    return jax.shard_map(shards, mesh=mesh, in_specs=in_specs, out_specs=out_specs, check_vma=False)
```

```python
import math

import jax
import jax.numpy as jnp
from jax import lax
from jax.sharding import Mesh
from jax.sharding import PartitionSpec as P

F32 = jnp.float32
BF16 = jnp.bfloat16
PLANE = ("replica", "tensor")
DP = ("run", "place")
LANES = 128


def dot(a, b, contract):
    return lax.dot_general(a, b, (contract, ((), ())), preferred_element_type=F32)


def exchange(x, axis):
    return lax.all_to_all(x, axis, split_axis=0, concat_axis=0, tiled=True)


def spread(x, axis):
    size = lax.axis_size(axis)
    return exchange(jnp.broadcast_to(x[None], (size,) + x.shape), axis)


def after(x, *others):
    return lax.optimization_barrier((x,) + others)[0]


def shift(x, by):
    size = lax.axis_size(DP)
    return lax.ppermute(x, DP, [(i, (i + by) % size) for i in range(size)])


def gather_dp(x):
    quad = lax.all_gather(x, "run", axis=0)
    return jnp.concatenate(
        [quad, shift(quad, 1), shift(quad, -1), shift(quad[0:2], -2), shift(quad[2:4], 2)],
        axis=0,
    )


def scatter_dp(x):
    half = x.shape[1] // 16 * 8
    run = lax.axis_index("run")
    one = shift(x[4:8], -1)
    two = shift(x[8:12], 1)
    three = shift(x[12:16], 2)
    quad = x[0:4].astype(F32) + one.astype(F32) + two.astype(F32) + three.astype(F32)
    near, above, far, below = (
        lax.dynamic_index_in_dim(quad, (run + k) % 4, 0, keepdims=False) for k in range(4)
    )
    far = far.astype(BF16)
    above_half = shift(far[:half], 4).astype(F32)
    below_half = shift(far[half:], -4).astype(F32)
    above = jnp.concatenate([above[:half] + above_half, above[half:]], axis=0).astype(BF16)
    below = jnp.concatenate([below[:half], below[half:] + below_half], axis=0).astype(BF16)
    return near + shift(above, 4).astype(F32) + shift(below, -4).astype(F32)


def normalize(residual, summed):
    combined = residual.astype(F32) + summed
    inverse = lax.rsqrt(jnp.sum(combined * combined, axis=1, keepdims=True) + 1e-06)
    return (combined * inverse, inverse)


def retract(normed, inverse, gradient):
    projection = jnp.sum(normed * gradient, axis=1, keepdims=True)
    return ((gradient - normed * projection) * inverse).astype(BF16)


def shards(
    image_residual_input,
    image_hidden_units,
    image_output_weight,
    text_residual_input,
    text_hidden_units,
    text_output_weight,
    log_logit_scale,
    pair_logit_bias,
):
    rows, width = image_residual_input.shape
    n_dp = lax.axis_size(DP)
    n_replica = lax.axis_size("replica")
    n_tensor = lax.axis_size("tensor")
    replica = lax.axis_index("replica")
    tensor = lax.axis_index("tensor")
    own = rows // n_tensor
    members = n_replica * n_tensor
    columns = width // n_replica

    terms = jnp.concatenate(
        [
            dot(image_hidden_units, image_output_weight, ((1,), (0,)))
            .astype(BF16)
            .reshape(n_tensor, own, width),
            dot(text_hidden_units, text_output_weight, ((1,), (0,)))
            .astype(BF16)
            .reshape(n_tensor, own, width),
        ],
        axis=1,
    )
    summed = jnp.sum(exchange(terms, "tensor").astype(F32), axis=0)
    image_residual = lax.dynamic_slice_in_dim(image_residual_input, tensor * own, own, 0)
    text_residual = lax.dynamic_slice_in_dim(text_residual_input, tensor * own, own, 0)
    normed_text, inverse_text = normalize(text_residual, summed[own:])
    normed_image, inverse_image = normalize(image_residual, summed[:own])

    hidden_image, hidden_text = (
        lax.all_gather(after(units, summed), "replica", axis=0, tiled=True)
        for units in (image_hidden_units, text_hidden_units)
    )

    images = spread(normed_image.astype(BF16), PLANE)
    texts = gather_dp(normed_text.astype(BF16))
    texts, images = lax.optimization_barrier((texts, images))
    texts = texts.reshape(n_dp * own, width)
    images = images.reshape(members * own, width)

    scale = jnp.exp(log_logit_scale[0])
    logits = scale * dot(images, texts, ((1,), (1,))) + pair_logit_bias[0]
    image_index = jnp.arange(members * own, dtype=jnp.int32)
    position = jnp.arange(n_dp * own, dtype=jnp.int32)
    text_index = jnp.where(
        position // own == lax.axis_index("run"),
        (replica * n_tensor + tensor) * own + position % own,
        -1,
    )
    label = jnp.where(image_index[:, None] == text_index[None, :], 1.0, -1.0).astype(F32)
    coefficients = (-label * jax.nn.sigmoid(-label * logits) * scale).astype(BF16)
    image_partial = dot(coefficients, texts, ((1,), (0,))).astype(BF16)
    coefficients, image_partial = lax.optimization_barrier((coefficients, image_partial))
    image_parts = exchange(image_partial.reshape(members, own, width), PLANE)
    text_partial = dot(coefficients, images, ((0,), (0,))).astype(BF16)
    text_grad = scatter_dp(text_partial.reshape(n_dp, own, width))
    image_grad = jnp.sum(image_parts.astype(F32), axis=0)

    upstream_image = retract(normed_image, inverse_image, image_grad)
    upstream_text = retract(normed_text, inverse_text, text_grad)
    cut = jnp.concatenate(
        [
            upstream_image.reshape(own, n_replica, columns),
            upstream_text.reshape(own, n_replica, columns),
        ],
        axis=2,
    )
    cut = exchange(jnp.transpose(cut, (1, 0, 2)), "replica")
    cut = lax.all_gather(cut, "tensor", axis=1).reshape(members * own, 2 * columns)
    group = after(jnp.stack([upstream_image, upstream_text]), cut)
    group = lax.all_gather(group, "tensor", axis=1)
    hidden_grad_image = dot(
        group[0].reshape(rows, width), image_output_weight, ((1,), (1,))
    ).astype(BF16)
    hidden_grad_text = dot(
        group[1].reshape(rows, width), text_output_weight, ((1,), (1,))
    ).astype(BF16)

    hidden = image_hidden_units.shape[1]
    side = lax.axis_size("run")
    partial = jnp.concatenate(
        [
            dot(cut, hidden_image, ((0,), (0,)))[:columns],
            dot(cut, hidden_text, ((0,), (0,)))[columns:],
        ],
        axis=0,
    ).astype(BF16)
    pieces = exchange(pack(partial, side), DP)
    share = jnp.sum(pieces.astype(F32), axis=0).astype(BF16)
    total = unpack(spread(share, DP), side, hidden).astype(F32)
    return (hidden_grad_image, hidden_grad_text, total[:columns].T, total[columns:].T)


def pack(x, side):
    size = side * side
    high = x.shape[0] // side
    whole = side * LANES
    blocks = [
        x[:, k * LANES : (k + 1) * LANES].reshape(side, high, LANES) for k in range(side)
    ]
    rest = [x[k * high : (k + 1) * high, whole:] for k in range(side)]
    rest = jnp.concatenate(rest, axis=1).reshape(high // 8, 8, LANES)
    rest = jnp.pad(rest, ((0, size - high // 8), (0, 0), (0, 0)))
    return jnp.concatenate([jnp.concatenate(blocks, axis=0), rest], axis=1)


def unpack(x, side, lanes):
    high = x.shape[1] - 8
    left = lanes - side * LANES
    blocks = [
        x[k * side : (k + 1) * side, :high].reshape(side * high, LANES) for k in range(side)
    ]
    rest = x[: high // 8, high:].reshape(high, LANES)
    rest = [rest[:, k * left : (k + 1) * left] for k in range(side)]
    return jnp.concatenate(blocks + [jnp.concatenate(rest, axis=0)], axis=1)


def solution(mesh):
    n_dp, n_replica, n_tensor = mesh.devices.shape
    n_run = math.isqrt(n_dp)
    mesh = Mesh(
        mesh.devices.reshape(n_run, n_dp // n_run, n_replica, n_tensor),
        ("run", "place", "replica", "tensor"),
    )
    rows = ("run", "place", "replica")
    in_specs = (
        P(rows, None),
        P(rows, "tensor"),
        P("tensor", None),
        P(rows, None),
        P(rows, "tensor"),
        P("tensor", None),
        P(),
        P(),
    )
    out_specs = (
        P(rows, "tensor"),
        P(rows, "tensor"),
        P("tensor", "replica"),
        P("tensor", "replica"),
    )
    return jax.shard_map(shards, mesh=mesh, in_specs=in_specs, out_specs=out_specs, check_vma=False)
```

```python
import math

import jax
import jax.numpy as jnp
from jax import lax
from jax.sharding import Mesh
from jax.sharding import PartitionSpec as P

F32 = jnp.float32
BF16 = jnp.bfloat16
PLANE = ("replica", "tensor")
DP = ("run", "place")
LANES = 128


def dot(a, b, contract):
    return lax.dot_general(a, b, (contract, ((), ())), preferred_element_type=F32)


def exchange(x, axis):
    return lax.all_to_all(x, axis, split_axis=0, concat_axis=0, tiled=True)


def spread(x, axis):
    size = lax.axis_size(axis)
    return exchange(jnp.broadcast_to(x[None], (size,) + x.shape), axis)


def after(x, *others):
    return lax.optimization_barrier((x,) + others)[0]


def shift(x, by):
    size = lax.axis_size(DP)
    return lax.ppermute(x, DP, [(i, (i + by) % size) for i in range(size)])


def gather_dp(x):
    quad = lax.all_gather(x, "run", axis=0)
    return jnp.concatenate(
        [quad, shift(quad, 1), shift(quad, -1), shift(quad[0:2], -2), shift(quad[2:4], 2)],
        axis=0,
    )


def scatter_dp(x):
    half = x.shape[1] // 16 * 8
    run = lax.axis_index("run")
    one = shift(x[4:8], -1)
    two = shift(x[8:12], 1)
    three = shift(x[12:16], 2)
    quad = x[0:4].astype(F32) + one.astype(F32) + two.astype(F32) + three.astype(F32)
    near, above, far, below = (
        lax.dynamic_index_in_dim(quad, (run + k) % 4, 0, keepdims=False) for k in range(4)
    )
    far = far.astype(BF16)
    above_half = shift(far[:half], 4).astype(F32)
    below_half = shift(far[half:], -4).astype(F32)
    above = jnp.concatenate([above[:half] + above_half, above[half:]], axis=0).astype(BF16)
    below = jnp.concatenate([below[:half], below[half:] + below_half], axis=0).astype(BF16)
    return near + shift(above, 4).astype(F32) + shift(below, -4).astype(F32)


def normalize(residual, summed):
    combined = residual.astype(F32) + summed
    inverse = lax.rsqrt(jnp.sum(combined * combined, axis=1, keepdims=True) + 1e-06)
    return (combined * inverse, inverse)


def retract(normed, inverse, gradient):
    projection = jnp.sum(normed * gradient, axis=1, keepdims=True)
    return ((gradient - normed * projection) * inverse).astype(BF16)


def shards(
    image_residual_input,
    image_hidden_units,
    image_output_weight,
    text_residual_input,
    text_hidden_units,
    text_output_weight,
    log_logit_scale,
    pair_logit_bias,
):
    rows, width = image_residual_input.shape
    n_dp = lax.axis_size(DP)
    n_replica = lax.axis_size("replica")
    n_tensor = lax.axis_size("tensor")
    replica = lax.axis_index("replica")
    tensor = lax.axis_index("tensor")
    own = rows // n_tensor
    members = n_replica * n_tensor
    columns = width // n_replica

    terms = jnp.concatenate(
        [
            dot(image_hidden_units, image_output_weight, ((1,), (0,)))
            .astype(BF16)
            .reshape(n_tensor, own, width),
            dot(text_hidden_units, text_output_weight, ((1,), (0,)))
            .astype(BF16)
            .reshape(n_tensor, own, width),
        ],
        axis=1,
    )
    summed = jnp.sum(exchange(terms, "tensor").astype(F32), axis=0)
    image_residual = lax.dynamic_slice_in_dim(image_residual_input, tensor * own, own, 0)
    text_residual = lax.dynamic_slice_in_dim(text_residual_input, tensor * own, own, 0)
    normed_text, inverse_text = normalize(text_residual, summed[own:])
    normed_image, inverse_image = normalize(image_residual, summed[:own])

    hidden_image, hidden_text = (
        lax.all_gather(after(units, summed), "replica", axis=0, tiled=True)
        for units in (image_hidden_units, text_hidden_units)
    )

    images = spread(normed_image.astype(BF16), PLANE)
    texts = gather_dp(normed_text.astype(BF16))
    texts, images = lax.optimization_barrier((texts, images))
    texts = texts.reshape(n_dp * own, width)
    images = images.reshape(members * own, width)

    scale = jnp.exp(log_logit_scale[0])
    logits = scale * dot(images, texts, ((1,), (1,))) + pair_logit_bias[0]
    image_index = jnp.arange(members * own, dtype=jnp.int32)
    position = jnp.arange(n_dp * own, dtype=jnp.int32)
    text_index = jnp.where(
        position // own == lax.axis_index("run"),
        (replica * n_tensor + tensor) * own + position % own,
        -1,
    )
    label = jnp.where(image_index[:, None] == text_index[None, :], 1.0, -1.0).astype(F32)
    coefficients = (-label * jax.nn.sigmoid(-label * logits) * scale).astype(BF16)
    image_partial = dot(coefficients, texts, ((1,), (0,))).astype(BF16)
    coefficients, image_partial = lax.optimization_barrier((coefficients, image_partial))
    image_parts = exchange(image_partial.reshape(members, own, width), PLANE)
    text_partial = dot(coefficients, images, ((0,), (0,))).astype(BF16)
    text_grad = scatter_dp(text_partial.reshape(n_dp, own, width))
    image_grad = jnp.sum(image_parts.astype(F32), axis=0)

    upstream_image = retract(normed_image, inverse_image, image_grad)
    upstream_text = retract(normed_text, inverse_text, text_grad)
    cut = jnp.concatenate(
        [
            upstream_image.reshape(own, n_replica, columns),
            upstream_text.reshape(own, n_replica, columns),
        ],
        axis=2,
    )
    cut = exchange(jnp.transpose(cut, (1, 0, 2)), "replica")
    cut, hidden_image, hidden_text = lax.optimization_barrier((cut, hidden_image, hidden_text))
    cut = lax.all_gather(cut, "tensor", axis=1).reshape(members * own, 2 * columns)
    group = after(jnp.stack([upstream_image, upstream_text]), cut)
    group = lax.all_gather(group, "tensor", axis=1)
    hidden_grad_image = dot(
        group[0].reshape(rows, width), image_output_weight, ((1,), (1,))
    ).astype(BF16)
    hidden_grad_text = dot(
        group[1].reshape(rows, width), text_output_weight, ((1,), (1,))
    ).astype(BF16)

    hidden = image_hidden_units.shape[1]
    side = lax.axis_size("run")
    partial = jnp.concatenate(
        [
            dot(cut, hidden_image, ((0,), (0,)))[:columns],
            dot(cut, hidden_text, ((0,), (0,)))[columns:],
        ],
        axis=0,
    ).astype(BF16)
    pieces = exchange(pack(partial, side), DP)
    share = jnp.sum(pieces.astype(F32), axis=0).astype(BF16)
    total = unpack(spread(share, DP), side, hidden).astype(F32)
    return (hidden_grad_image, hidden_grad_text, total[:columns].T, total[columns:].T)


def pack(x, side):
    size = side * side
    high = x.shape[0] // side
    whole = side * LANES
    blocks = [
        x[:, k * LANES : (k + 1) * LANES].reshape(side, high, LANES) for k in range(side)
    ]
    rest = [x[k * high : (k + 1) * high, whole:] for k in range(side)]
    rest = jnp.concatenate(rest, axis=1).reshape(high // 8, 8, LANES)
    rest = jnp.pad(rest, ((0, size - high // 8), (0, 0), (0, 0)))
    return jnp.concatenate([jnp.concatenate(blocks, axis=0), rest], axis=1)


def unpack(x, side, lanes):
    high = x.shape[1] - 8
    left = lanes - side * LANES
    blocks = [
        x[k * side : (k + 1) * side, :high].reshape(side * high, LANES) for k in range(side)
    ]
    rest = x[: high // 8, high:].reshape(high, LANES)
    rest = [rest[:, k * left : (k + 1) * left] for k in range(side)]
    return jnp.concatenate(blocks + [jnp.concatenate(rest, axis=0)], axis=1)


def solution(mesh):
    n_dp, n_replica, n_tensor = mesh.devices.shape
    n_run = math.isqrt(n_dp)
    mesh = Mesh(
        mesh.devices.reshape(n_run, n_dp // n_run, n_replica, n_tensor),
        ("run", "place", "replica", "tensor"),
    )
    rows = ("run", "place", "replica")
    in_specs = (
        P(rows, None),
        P(rows, "tensor"),
        P("tensor", None),
        P(rows, None),
        P(rows, "tensor"),
        P("tensor", None),
        P(),
        P(),
    )
    out_specs = (
        P(rows, "tensor"),
        P(rows, "tensor"),
        P("tensor", "replica"),
        P("tensor", "replica"),
    )
    return jax.shard_map(shards, mesh=mesh, in_specs=in_specs, out_specs=out_specs, check_vma=False)
```
